32 devices in a mesh: fsdp: 8 (over z, y), frame: 4 (over x, core).
Axes of the slice: x: 2, y: 2, z: 4, core: 2. Of those that a mesh axis runs over, the one named last changes fastest.
Arguments:
- latents: bfloat16 [2, 8, 8, 128, 16], P(None, 'fsdp', 'frame'), may hold values from -6 to 6
- added_noise: bfloat16 [2, 8, 8, 128, 16], P(None, 'fsdp', 'frame'), may hold values from -6 to 6
- text_states: bfloat16 [2, 8, 64, 4096], P(None, 'fsdp'), may hold values from -1.75 to 1.75
- timesteps: int32 [2, 8], P(None, 'fsdp'), may hold values from 1 to 999
- token_counts: int32 [2, 8], P(None, 'fsdp'), may hold values from 26 to 128, as said below
- frame_counts: int32 [2, 8, 3], P(None, 'fsdp'), may hold values from 1 to 5, 8 in all within a row
- w_shared: float32 [1152, 12448], P('fsdp'), may hold values from -0.1875 to 0.1875
- w_spatial: float32 [1152, 18432], P('fsdp'), may hold values from -0.1875 to 0.1875
- w_temporal: float32 [1152, 13824], P('fsdp'), may hold values from -0.1875 to 0.1875
- shift_tables: float32 [1152, 14], P('fsdp'), may hold values from -3 to 3
- m_shared: float32 [1152, 12448], P('fsdp'), may hold values from -9.536743e-07 to 9.536743e-07
- m_spatial: float32 [1152, 18432], P('fsdp'), may hold values from -9.536743e-07 to 9.536743e-07
- m_temporal: float32 [1152, 13824], P('fsdp'), may hold values from -9.536743e-07 to 9.536743e-07
- m_tables: float32 [1152, 14], P('fsdp'), may hold values from -9.536743e-07 to 9.536743e-07
- v_shared: float32 [1152, 12448], P('fsdp'), may hold values from 1.941177e-15 to 7.764708e-15
- v_spatial: float32 [1152, 18432], P('fsdp'), may hold values from 1.941177e-15 to 7.764708e-15
- v_temporal: float32 [1152, 13824], P('fsdp'), may hold values from 1.941177e-15 to 7.764708e-15
- v_tables: float32 [1152, 14], P('fsdp'), may hold values from 1.941177e-15 to 7.764708e-15
Outputs:
- loss_sum: float32 [], replicated
- weight_total: float32 [], replicated
- grad_norm: float32 [], replicated
- matrix_norms: float32 [2, 18], replicated
- clipped_norms: float32 [18], replicated
- new_shared: float32 [1152, 12448], P('fsdp')
- new_spatial: float32 [1152, 18432], P('fsdp')
- new_temporal: float32 [1152, 13824], P('fsdp')
- new_tables: float32 [1152, 14], P('fsdp')
- first_shared: float32 [1152, 12448], P('fsdp')
- first_spatial: float32 [1152, 18432], P('fsdp')
- first_temporal: float32 [1152, 13824], P('fsdp')
- first_tables: float32 [1152, 14], P('fsdp')
- second_shared: float32 [1152, 12448], P('fsdp')
- second_spatial: float32 [1152, 18432], P('fsdp')
- second_temporal: float32 [1152, 13824], P('fsdp')
- second_tables: float32 [1152, 14], P('fsdp')
- copy_shared: bfloat16 [1152, 12448], P('fsdp')
- copy_spatial: bfloat16 [1152, 18432], P('fsdp')
- copy_temporal: bfloat16 [1152, 13824], P('fsdp')
- copy_tables: bfloat16 [1152, 14], P('fsdp')
The draws below stay inside these ranges and needn't reach their ends.
Inputs may be any that keep to these rules, and one draw needn't show every extreme that they name: `token_counts`: valid patch tokens of each frame of a video; the rest of its 128 rows are padding. `frame_counts`: frames of the clips packed into a video, in order; they sum to 8.
All inputs are finite; a program needn't handle non-finite values.
Results may differ from the reference program's by a relative error of at most 0.0088.
Values may be sent and summed in bfloat16 or wider, within the bound.
No kernel may reach another device: no remote copies, remote signals or barrier semaphores. Data moves between devices by JAX's collectives and lax.ppermute only.
A program may use at most 768 MiB of HBM per device.

```python
import math
import jax
import jax.numpy as jnp
import numpy as np
from jax import lax

D = 1152
HEADS = 16
HEAD_DIM = 72
FF = 4608
TXT_D = 4096
FREQ = 256
PCH = 16
S = 128
FD = 2
TXT = 64
MICRO = 2
CLIPS = 3
STEP = 10
VIDS = 8
F = 8
NPAR = 51515136
N_FRAME = 4


def draw_token_counts(key, part):
    key = jax.random.fold_in(key, 7)
    position = jnp.arange(VIDS, dtype=jnp.int32)
    lower = S // 3
    rising = lower + (S - lower) * position // (VIDS - 1)
    jitter = jax.random.randint(key, (MICRO, VIDS), 0, S // 8 + 1)
    counts = jnp.clip(rising[None, :] - jitter, 1, S)
    return jnp.where(position[None, :] == VIDS - 1, S, counts).astype(jnp.int32)


def place_ends(array, own_key, low, top_value):
    index_at = [jax.random.randint(jax.random.fold_in(own_key, axis), (), 0, length) for axis, length in enumerate(array.shape)]
    longest = array.shape.index(max(array.shape))
    beside = index_at[:longest] + [(index_at[longest] + 1) % array.shape[longest]] + index_at[longest + 1:]
    return array.at[tuple(index_at)].set(low).at[tuple(beside)].set(top_value)


def steps_of(rng, extent, cuts, low, high):
    def one(dim, blocks):
        draws = jax.random.uniform(jax.random.fold_in(jax.random.fold_in(rng, 6), dim), (blocks,), jnp.float32, low / len(cuts), high / len(cuts))
        return jnp.repeat(jnp.exp(draws), extent[dim] // blocks).reshape((-1,) + (1,) * (len(extent) - dim - 1))

    factor_of = one(*cuts[0])
    for cut in cuts[1:]:
        factor_of = factor_of * one(*cut)
    return factor_of


def length_profile(count, total, limit, lean):
    portions = [(1 << 20) // math.isqrt(grade ** lean) + 1 for grade in range(2, count + 1)]
    surplus, given = total - limit - (count - 1), [1] * (count - 1)
    while surplus > 0:
        movable = [i for i in range(count - 1) if given[i] < limit]
        pool, budget = sum([portions[i] for i in movable]), surplus
        for i in movable:
            addition = min(limit - given[i], max(1, budget * portions[i] // pool), surplus)
            given[i] = given[i] + addition
            surplus = surplus - addition
    return np.array([limit] + given)


def uneven(key, count, total, bound, skew):
    if count == 2:
        one = jax.random.randint(key, (), max(1, total - bound), min(bound, total - 1) + 1)
        return jnp.stack([one, total - one])
    sizes = jnp.asarray(length_profile(count, total, bound, skew), jnp.int32)
    pairs = (count - 1) // 2
    giver, receiver = sizes[1:1 + 2 * pairs:2], sizes[2:2 + 2 * pairs:2]
    margin = jnp.minimum(giver - 1, bound - receiver)
    shifted = jax.random.randint(jax.random.fold_in(key, 1), (pairs,), 0, 1 << 20) % (margin + 1)
    sizes = sizes.at[1:1 + 2 * pairs:2].set(giver - shifted).at[2:2 + 2 * pairs:2].set(receiver + shifted)
    return sizes[jax.random.permutation(jax.random.fold_in(key, 2), count)]


def bell_draw(own_key, dims, scale, most, cuts=(), held_as=jnp.bfloat16):
    entries = scale * jax.random.normal(own_key, dims, jnp.float32)
    if cuts:
        entries = entries * steps_of(own_key, dims, cuts, -0.22, 0.18)
    return jnp.clip(entries, -most, most).astype(held_as)


def setup_inputs(seed: int = 0) -> dict:
    splits = jax.random.split(jax.random.key(seed), 19)
    return {
        "latents": bell_draw(splits[0], (MICRO, VIDS, F, S, PCH), 1.0, 6.0, ((1, 8), (2, 4))),
        "added_noise": bell_draw(splits[1], (MICRO, VIDS, F, S, PCH), 1.0, 6.0, ((1, 8), (2, 4))),
        "text_states": bell_draw(splits[2], (MICRO, VIDS, TXT, TXT_D), 0.3, 1.75, ((1, 8),)),
        "timesteps": place_ends(jax.random.randint(splits[3], (MICRO, VIDS), 1, 1000), jax.random.fold_in(splits[3], 1), 1, 999).astype(jnp.int32),
        "token_counts": draw_token_counts(jax.random.fold_in(splits[18], 71), 0),
        "frame_counts": jax.vmap(lambda own: uneven(own, CLIPS, F, F - 3, 0))(jax.random.split(splits[5], MICRO * VIDS)).reshape((MICRO, VIDS, CLIPS)).astype(jnp.int32),
        "w_shared": bell_draw(splits[6], (D, 2 * PCH + FREQ + TXT_D + 7 * D), D ** -0.5, 0.1875, ((0, 8),), jnp.float32),
        "w_spatial": bell_draw(splits[7], (D, 8 * D + 2 * FF), D ** -0.5, 0.1875, ((0, 8),), jnp.float32),
        "w_temporal": bell_draw(splits[8], (D, 4 * D + 2 * FF), D ** -0.5, 0.1875, ((0, 8),), jnp.float32),
        "shift_tables": bell_draw(splits[9], (D, 14), 0.5, 3.0, ((0, 8),), jnp.float32),
        "m_shared": bell_draw(splits[10], (D, 2 * PCH + FREQ + TXT_D + 7 * D), (0.0011 / NPAR ** 0.5), 9.5367431640625e-07, ((0, 8),), jnp.float32),
        "m_spatial": bell_draw(splits[11], (D, 8 * D + 2 * FF), (0.0011 / NPAR ** 0.5), 9.5367431640625e-07, ((0, 8),), jnp.float32),
        "m_temporal": bell_draw(splits[12], (D, 4 * D + 2 * FF), (0.0011 / NPAR ** 0.5), 9.5367431640625e-07, ((0, 8),), jnp.float32),
        "m_tables": bell_draw(splits[13], (D, 14), (0.0011 / NPAR ** 0.5), 9.5367431640625e-07, ((0, 8),), jnp.float32),
        "v_shared": jnp.clip(jnp.exp(math.log(7.764707828799861e-15) - 1.3862944 * jax.random.uniform(splits[14], (D, 2 * PCH + FREQ + TXT_D + 7 * D), jnp.float32) ** steps_of(splits[14], (D, 2 * PCH + FREQ + TXT_D + 7 * D), ((0, 8),), -0.2, 0.2)), 1.9411769571999653e-15, 7.764707828799861e-15),
        "v_spatial": jnp.clip(jnp.exp(math.log(7.764707828799861e-15) - 1.3862944 * jax.random.uniform(splits[15], (D, 8 * D + 2 * FF), jnp.float32) ** steps_of(splits[15], (D, 8 * D + 2 * FF), ((0, 8),), -0.2, 0.2)), 1.9411769571999653e-15, 7.764707828799861e-15),
        "v_temporal": jnp.clip(jnp.exp(math.log(7.764707828799861e-15) - 1.3862944 * jax.random.uniform(splits[16], (D, 4 * D + 2 * FF), jnp.float32) ** steps_of(splits[16], (D, 4 * D + 2 * FF), ((0, 8),), -0.2, 0.2)), 1.9411769571999653e-15, 7.764707828799861e-15),
        "v_tables": jnp.clip(jnp.exp(math.log(7.764707828799861e-15) - 1.3862944 * jax.random.uniform(splits[17], (D, 14), jnp.float32) ** steps_of(splits[17], (D, 14), ((0, 8),), -0.2, 0.2)), 1.9411769571999653e-15, 7.764707828799861e-15),
    }


@jax.custom_vjp
def low(v):
    return lax.optimization_barrier(v.astype(jnp.bfloat16)).astype(jnp.float32)

@jax.custom_vjp
def low_back(v):
    return v

def low_keep(v):
    return (low(v), None)

def low_pass(kept, grad):
    return (grad,)

def back_keep(v):
    return (v, None)

def back_low(kept, grad):
    return (low(grad),)
low.defvjp(low_keep, low_pass)
low_back.defvjp(back_keep, back_low)
PRECISE = lax.Precision.HIGHEST
CLIP_NORM = 0.01
LEARN_RATE = 0.3
BETA_ONE = 0.9
BETA_TWO = 0.999
ADAM_EPS = 1e-06
DECAY_RATE = 0.01
SNR_GAMMA = 5.0
NORM_EPS = 1e-06

def matmul_low(inputs, weight):
    return low_back(jnp.matmul(low(inputs), weight, precision=PRECISE))

def layer_norm(values):
    centered = values - lax.optimization_barrier(jnp.mean(values, axis=-1, keepdims=True))
    return centered * lax.rsqrt(lax.optimization_barrier(jnp.mean(centered * centered, axis=-1, keepdims=True)) + NORM_EPS)

def modulate(residual, shift_by, scale_by):
    return layer_norm(residual) * (1.0 + scale_by) + shift_by

def gelu_tanh(values):
    return jax.nn.gelu(values, approximate=True)

def split_heads(values):
    return values.reshape(values.shape[:-1] + (HEADS, HEAD_DIM))

def join_heads(values):
    return values.reshape(values.shape[:-2] + (HEADS * HEAD_DIM,))

def shared_widths():
    return (PCH, FREQ, TXT_D, D, 6 * D, PCH)

def spatial_widths():
    return (3 * D, D, D, 2 * D, D, FF, FF)

def temporal_widths():
    return (3 * D, D, FF, FF)

def split_columns(weight, widths):
    pieces = []
    offset = 0
    for column_count in widths:
        pieces.append(weight[:, offset:offset + column_count])
        offset += column_count
    return pieces

def spread_columns(values, widths):
    return jnp.concatenate([jnp.full((column_count,), values[position]) for position, column_count in enumerate(widths)])

def matrix_squares(arrays):
    totals = []
    for array_one, widths in zip(arrays[:3], (shared_widths(), spatial_widths(), temporal_widths())):
        for column_block in split_columns(array_one, widths):
            totals.append(jnp.sum(column_block * column_block))
    totals.append(jnp.sum(arrays[3] * arrays[3]))
    return jnp.stack(totals)

def attend(query_heads, key_heads, value_heads, allowed):
    scores = low_back(jnp.einsum('...qhd,...khd->...hqk', low(query_heads), low(key_heads), precision=PRECISE))
    scores = jnp.where(allowed, scores * (1.0 / math.sqrt(HEAD_DIM)), -1e+30)
    soft_weights = jax.nn.softmax(scores, axis=-1)
    return low_back(jnp.einsum('...hqk,...khd->...qhd', low(soft_weights), low(value_heads), precision=PRECISE))

def block(residual, six_rows, matrices, allowed, cross, temporal):
    gate_parts = [six_rows[:, position][:, None, :] for position in range(6)]
    packed = matmul_low(modulate(residual, gate_parts[0], gate_parts[1]), matrices[0])
    query_heads = split_heads(packed[..., :D])
    key_heads = split_heads(packed[..., D:2 * D])
    value_heads = split_heads(packed[..., 2 * D:])
    if temporal:
        mixed_heads = jnp.swapaxes(attend(jnp.swapaxes(query_heads, 0, 1), jnp.swapaxes(key_heads, 0, 1), jnp.swapaxes(value_heads, 0, 1), allowed), 0, 1)
    else:
        mixed_heads = attend(query_heads, key_heads, value_heads, allowed)
    residual = residual + gate_parts[2] * matmul_low(join_heads(mixed_heads), matrices[1])
    if cross is not None:
        cross_query = split_heads(matmul_low(residual, cross[0]))
        residual = residual + matmul_low(join_heads(attend(cross_query, cross[2], cross[3], True)), cross[1])
    hidden = gelu_tanh(matmul_low(modulate(residual, gate_parts[3], gate_parts[4]), matrices[2]))
    return residual + gate_parts[5] * matmul_low(hidden, matrices[3].T)

def video_loss(matrices, video_item):
    shared, spatial, temporal, tables = matrices
    clean_latent, target, text_item, step_item, token_count, lengths = video_item
    step_float = step_item.astype(jnp.float32)
    alpha_bar = jnp.cos((step_float / 1000.0 + 0.008) / 1.008 * (math.pi / 2)) ** 2
    noisy = jnp.sqrt(alpha_bar) * clean_latent + jnp.sqrt(1.0 - alpha_bar) * target
    patches_in = matmul_low(noisy, shared[0].T)
    half_count = FREQ // 2
    frequency = jnp.exp(-math.log(10000.0) * jnp.arange(half_count, dtype=jnp.float32) / half_count)
    angles = step_float * frequency
    features = jnp.concatenate([jnp.cos(angles), jnp.sin(angles)])

    def condition(unused):
        embedding = matmul_low(jax.nn.silu(matmul_low(features, shared[1].T)), shared[3])
        modulation = matmul_low(jax.nn.silu(embedding), shared[4])
        caption = gelu_tanh(matmul_low(text_item, shared[2].T))
        return (embedding, modulation, matmul_low(caption, spatial[3]))
    embedding, modulation, cross_pair = lax.map(condition, jnp.arange(N_FRAME))
    six_spatial = jnp.repeat(modulation.reshape(N_FRAME, 6, D) + tables[:, 0:6].T, FD, axis=0)
    six_temporal = jnp.repeat(modulation.reshape(N_FRAME, 6, D) + tables[:, 6:12].T, FD, axis=0)
    final_rows = jnp.repeat(embedding[:, None, :] + tables[:, 12:14].T, FD, axis=0)
    cross_keys = jnp.repeat(split_heads(cross_pair[..., :D]), FD, axis=0)
    cross_values = jnp.repeat(split_heads(cross_pair[..., D:]), FD, axis=0)
    key_valid = jnp.arange(S) < token_count
    clip_ends = jnp.cumsum(lengths)
    segment = lax.optimization_barrier(jnp.sum((jnp.arange(F)[:, None] >= clip_ends[None, :]).astype(jnp.int32), axis=-1))
    same_clip = segment[:, None] == segment[None, :]
    hidden = block(patches_in, six_spatial, (spatial[0], spatial[1], spatial[5], spatial[6]), key_valid, (spatial[2], spatial[4], cross_keys, cross_values), False)
    hidden = block(hidden, six_temporal, tuple(temporal), same_clip, None, True)
    predicted = matmul_low(modulate(hidden, final_rows[:, None, 0], final_rows[:, None, 1]), shared[5])
    pred_error = predicted - target
    snr_value = alpha_bar / (1.0 - alpha_bar)
    loss_weight = jnp.minimum(snr_value, SNR_GAMMA) / snr_value
    return loss_weight * jnp.sum(jnp.where(key_valid[None, :], lax.optimization_barrier(jnp.mean(pred_error * pred_error, axis=-1)), 0.0))

def reference(latents, added_noise, text_states, timesteps, token_counts, frame_counts, w_shared, w_spatial, w_temporal, shift_tables, m_shared, m_spatial, m_temporal, m_tables, v_shared, v_spatial, v_temporal, v_tables):
    videos_all = MICRO * VIDS
    items = (latents.reshape((videos_all,) + latents.shape[2:]).astype(jnp.float32), added_noise.reshape((videos_all,) + added_noise.shape[2:]).astype(jnp.float32), text_states.reshape((videos_all,) + text_states.shape[2:]).astype(jnp.float32), timesteps.reshape(videos_all), token_counts.reshape(videos_all), frame_counts.reshape(videos_all, CLIPS))
    masters = (w_shared, w_spatial, w_temporal, shift_tables)

    def total_loss(shared_w, spatial_w, temporal_w, tables_w):
        matrices = (split_columns(low(shared_w), shared_widths()), split_columns(low(spatial_w), spatial_widths()), split_columns(low(temporal_w), temporal_widths()), low(tables_w))

        def add_video(running, video_item):
            return (running + video_loss(matrices, video_item), None)
        return lax.scan(jax.checkpoint(add_video), jnp.zeros((), jnp.float32), items)[0]
    loss_sum, pullback = jax.vjp(total_loss, w_shared, w_spatial, w_temporal, shift_tables)
    grads = pullback(jnp.ones((), jnp.float32))
    step_float = timesteps.astype(jnp.float32)
    alpha_bar = jnp.cos((step_float / 1000.0 + 0.008) / 1.008 * (math.pi / 2)) ** 2
    snr_value = alpha_bar / (1.0 - alpha_bar)
    weight_all = jnp.minimum(snr_value, SNR_GAMMA) / snr_value
    weight_total = jnp.sum(weight_all * token_counts.astype(jnp.float32)) * F
    grad_sq = matrix_squares(grads)
    weight_sq = matrix_squares(masters)
    grad_norm = jnp.sqrt(jnp.sum(grad_sq)) / weight_total
    factor = CLIP_NORM / jnp.maximum(grad_norm, CLIP_NORM)
    grad_scale = factor / weight_total
    firsts, seconds, updates = ([], [], [])
    for grad_one, first_old, second_old, master in zip(grads, (m_shared, m_spatial, m_temporal, m_tables), (v_shared, v_spatial, v_temporal, v_tables), masters):
        clipped = grad_one * grad_scale
        first_new = BETA_ONE * first_old + (1.0 - BETA_ONE) * clipped
        second_new = BETA_TWO * second_old + (1.0 - BETA_TWO) * clipped * clipped
        updates.append(first_new / (1.0 - BETA_ONE ** STEP) / (jnp.sqrt(second_new / (1.0 - BETA_TWO ** STEP)) + ADAM_EPS) + DECAY_RATE * master)
        firsts.append(first_new)
        seconds.append(second_new)
    update_sq = matrix_squares(updates)
    trust_ratio = jnp.sqrt(weight_sq) / jnp.sqrt(update_sq)
    column_trust = (spread_columns(trust_ratio[0:6], shared_widths())[None, :], spread_columns(trust_ratio[6:13], spatial_widths())[None, :], spread_columns(trust_ratio[13:17], temporal_widths())[None, :], trust_ratio[17])
    new_values = [master - LEARN_RATE * trust_one * update for master, trust_one, update in zip(masters, column_trust, updates)]
    matrix_norms = jnp.stack([jnp.sqrt(weight_sq), jnp.sqrt(update_sq)])
    clipped_norms = jnp.sqrt(grad_sq) * grad_scale
    return (loss_sum, weight_total, grad_norm, matrix_norms, clipped_norms, new_values[0], new_values[1], new_values[2], new_values[3], firsts[0], firsts[1], firsts[2], firsts[3], seconds[0], seconds[1], seconds[2], seconds[3], new_values[0].astype(jnp.bfloat16), new_values[1].astype(jnp.bfloat16), new_values[2].astype(jnp.bfloat16), new_values[3].astype(jnp.bfloat16))
```

```python
import math

import jax
import jax.numpy as jnp
import numpy as np
from jax import lax
from jax.experimental import pallas as pl
from jax.experimental.pallas import tpu as pltpu
from jax.sharding import PartitionSpec as P

D = 1152
HEADS = 16
HEAD_DIM = 72
FF = 4608
TXT_D = 4096
FREQ = 256
PCH = 16
STEP = 10

CLIP_NORM = 0.01
LEARN_RATE = 0.3
BETA_ONE = 0.9
BETA_TWO = 0.999
ADAM_EPS = 1e-06
DECAY_RATE = 0.01
SNR_GAMMA = 5.0
NORM_EPS = 1e-06

F32 = jnp.float32
BF16 = jnp.bfloat16


def few(axis):
    return lax.axis_size(axis) <= 8


def swap(values, axis, mask):
    return lax.ppermute(values, axis, [(n, n ^ mask) for n in range(lax.axis_size(axis))])


def order_of(axis):
    return jnp.arange(lax.axis_size(axis), dtype=jnp.int32) ^ lax.axis_index(axis)


def to_relative(stacked, axis):
    return jnp.take(stacked, order_of(axis), axis=0)


def masks(axis):
    return [m for m in (2, 4, 1) if m < lax.axis_size(axis)] if axis == "fsdp" else [1, 2]


def gate(values, after):
    return lax.optimization_barrier((values, after))[0]


def sum_over(values, axis):
    if not few(axis):
        return lax.psum(values, axis)
    for mask in masks(axis):
        values = values + swap(values, axis, mask)
    return values


def sum_over_frame_low(values):
    for mask in (1, 2):
        low = values.astype(BF16)
        values = low.astype(F32) + swap(low, "frame", mask).astype(F32)
    return values


def collect(values, axis):
    if not few(axis):
        return to_relative(lax.all_gather(values, axis, axis=0), axis)
    blocks = values[None]
    for mask in masks(axis):
        blocks = jnp.concatenate([blocks, swap(blocks, axis, mask)])
    if axis == "frame":
        return blocks
    size = lax.axis_size(axis)
    return jnp.swapaxes(blocks.reshape((2, size // 2) + values.shape), 0, 1).reshape(blocks.shape)


def collect_along(values):
    if not few("fsdp"):
        return values
    size = lax.axis_size("fsdp")
    return jnp.stack([values] + [swap(values, "fsdp", mask) for mask in range(2, size, 2)])


def collect_beside(along):
    if not few("fsdp"):
        return collect(along, "fsdp")
    both = jnp.stack([along, swap(along, "fsdp", 1)], axis=1)
    return both.reshape((-1,) + along.shape[1:])


def deliver_beside(blocks):
    if not few("fsdp"):
        return blocks
    pairs = blocks.reshape((-1, 2) + blocks.shape[1:])
    return pairs[:, 0] + swap(pairs[:, 1], "fsdp", 1)


def deliver_along(half):
    if not few("fsdp"):
        return deliver(half, "fsdp")
    total = half[0]
    for k in range(1, half.shape[0]):
        total = total + swap(half[k], "fsdp", 2 * k)
    return total


def fence(values):
    flat = values.reshape(-1, values.shape[-1])
    return swap(flat[:8, :128], "frame", 1)


def deliver(blocks, axis):
    size = lax.axis_size(axis)
    if not few(axis):
        return lax.psum_scatter(to_relative(blocks, axis), axis, scatter_dimension=0).astype(F32)
    kind = blocks.dtype
    held = list(range(size))
    for mask in masks(axis)[::-1]:
        keep = [k for k in held if not k & mask]
        low = blocks.astype(kind)
        received = swap(jnp.stack([low[held.index(k ^ mask)] for k in keep]), axis, mask)
        blocks = jnp.stack([blocks[held.index(k)] for k in keep]).astype(F32)
        blocks = blocks + received.astype(F32)
        held = keep
    return blocks[0]


def sum_relative(blocks, axis):
    size = lax.axis_size(axis)
    if not few(axis):
        return to_relative(lax.psum(to_relative(blocks, axis), axis), axis)
    for mask in masks(axis):
        received = swap(blocks, axis, mask)
        blocks = blocks + jnp.stack([received[k ^ mask] for k in range(size)])
    return blocks


def layer_norm(values):
    centered = values - jnp.mean(values, axis=-1, keepdims=True)
    return centered * lax.rsqrt(jnp.mean(centered * centered, axis=-1, keepdims=True) + NORM_EPS)


def modulate(residual, shift_by, scale_by):
    return layer_norm(residual) * (1.0 + scale_by) + shift_by


def gelu_tanh(values):
    return jax.nn.gelu(values, approximate=True)


def shared_widths():
    return (PCH, FREQ, TXT_D, D, 6 * D, PCH)


def spatial_widths():
    return (3 * D, D, D, 2 * D, D, FF, FF)


def temporal_widths():
    return (3 * D, D, FF, FF)


def split_columns(weight, widths):
    pieces = []
    offset = 0
    for column_count in widths:
        pieces.append(weight[:, offset : offset + column_count])
        offset += column_count
    return pieces


def dot(left, right):
    return lax.dot_general(
        left,
        right,
        (((left.ndim - 1,), (0,)), ((), ())),
        preferred_element_type=F32,
    )


def dot_t(left, right):
    return lax.dot_general(
        left,
        right,
        (((left.ndim - 1,), (1,)), ((), ())),
        preferred_element_type=F32,
    )


def outer(left, right):
    return lax.dot_general(
        left.reshape(-1, left.shape[-1]),
        right.reshape(-1, right.shape[-1]),
        (((0,), (0,)), ((), ())),
        preferred_element_type=F32,
    )


def modulate_back(residual, shift_by, scale_by, grad):
    grad_residual, grad_shift, grad_scale = jax.vjp(modulate, residual, shift_by, scale_by)[1](grad)
    return grad_residual, grad_shift[:, 0], grad_scale[:, 0]


LINES = 4
QUERIES = 128
BLOCK = D // (2 * LINES)
VMEM_LIMIT = 58 * 2**20
SCALE = 1.0 / math.sqrt(HEAD_DIM)


def nn(left, right):
    return lax.dot_general(left, right, (((1,), (0,)), ((), ())), preferred_element_type=F32)


def nt(left, right):
    return lax.dot_general(left, right, (((1,), (1,)), ((), ())), preferred_element_type=F32)


def tn(left, right):
    return lax.dot_general(left, right, (((0,), (0,)), ((), ())), preferred_element_type=F32)


class Pieces:
    def __init__(self, plan, place, refs, dest, sems, indices):
        z, y = place[0], place[1]
        self.copies = []
        for n, index in enumerate(indices):
            for k in range(LINES):
                for m, column in enumerate((y, 1 - y)):
                    ref, entry = plan[2 * n + m]
                    row = pl.multiple_of((jnp.bitwise_xor(z, k) * 2 + column) * BLOCK, BLOCK)
                    self.copies.append(
                        pltpu.make_async_copy(
                            refs[ref].at[entry, k],
                            dest.at[index, pl.ds(row, BLOCK)],
                            sems.at[n, 2 * k + m],
                        )
                    )

    def start(self):
        @pl.when(pl.program_id(0) == 0)
        def _():
            for copy in self.copies:
                copy.start()

    def wait(self, first, count):
        @pl.when(pl.program_id(0) == 0)
        def _():
            for copy in self.copies[2 * LINES * first : 2 * LINES * (first + count)]:
                copy.wait()


def windows():
    for head in range(HEADS):
        first = head * HEAD_DIM
        start = first // 128 * 128
        yield first - start, start, (256 if first - start + HEAD_DIM > 128 else 128)


def head_mask(offset, width):
    lane = lax.broadcasted_iota(jnp.int32, (1, width), 1)
    return jnp.where((lane >= offset) & (lane < offset + HEAD_DIM), 1.0, 0.0).astype(BF16)


def soft_columns(scores, allowed):
    scores = scores * SCALE
    if allowed is not None:
        scores = jnp.where(allowed > 0.5, scores, -1e30)
    grown = jnp.exp(scores - jnp.max(scores, axis=0, keepdims=True))
    return grown / jnp.sum(grown, axis=0, keepdims=True)


def attend_rows(query, key, value, out, allowed):
    for offset, start, width in windows():
        mask = head_mask(offset, width)
        lanes = slice(start, start + width)
        soft = soft_columns(nt(key[:, lanes], query[:, lanes] * mask), allowed)
        out[:, lanes] += tn(soft.astype(BF16), value[:, lanes] * mask)


def attend_rows_back(query, key, value, grad, grad_query, grad_key, grad_value, allowed):
    for offset, start, width in windows():
        mask = head_mask(offset, width)
        lanes = slice(start, start + width)
        query_head = query[:, lanes] * mask
        key_head = key[:, lanes] * mask
        grad_head = grad[:, lanes] * mask
        soft = soft_columns(nt(key_head, query_head), allowed)
        grad_soft = nt(value[:, lanes], grad_head)
        grad_value[:, lanes] += nn(soft.astype(BF16), grad_head)
        grad_scores = soft * (grad_soft - jnp.sum(soft * grad_soft, axis=0, keepdims=True))
        grad_scores = (grad_scores * SCALE).astype(BF16)
        grad_key[:, lanes] += nn(grad_scores, query_head)
        grad_query[:, lanes] += tn(grad_scores, key_head)


def normal(values):
    centered = values - jnp.mean(values, axis=-1, keepdims=True)
    scale = lax.rsqrt(jnp.mean(centered * centered, axis=-1, keepdims=True) + NORM_EPS)
    return centered * scale, scale


def normal_back(normed, scale, grad):
    return scale * (
        grad
        - jnp.mean(grad, axis=-1, keepdims=True)
        - normed * jnp.mean(grad * normed, axis=-1, keepdims=True)
    )


def gelu_parts(values):
    root = math.sqrt(2.0 / math.pi)
    square = values * values
    bent = jnp.tanh(root * (values + 0.044715 * (values * square)))
    half = 0.5 * (1.0 + bent)
    slope = half + 0.5 * values * (1.0 - bent * bent) * (root * (1.0 + 3 * 0.044715 * square))
    return values * half, slope


def attention_kernel(cross, plan, place, rows6, x, allowed, *refs):
    if cross:
        pair, refs = refs[0], refs[1:]
    count = max(ref for ref, _ in plan) + 1
    weights, refs = refs[:count], refs[count:]
    if cross:
        (middle, packed, projected, lefts, cross_query) = refs[:5]
        refs = refs[5:]
        after_low, cross_mixed = lefts.at[:, :, 2 * D : 3 * D], lefts.at[:, :, 3 * D : 4 * D]
    else:
        (middle, packed, projected, lefts) = refs[:4]
        refs = refs[4:]
    normed, mixed = lefts.at[:, :, 0:D], lefts.at[:, :, D : 2 * D]
    dest, sems, total = refs
    j = place[2]
    indices = [jnp.bitwise_xor(j, k) for k in range(4)]
    if cross:
        c = jnp.bitwise_and(j, 1)
        indices += [4 + c, 5 - c]
    pieces = Pieces(plan, place, weights, dest, sems, indices)
    pieces.start()
    row = [rows6[0, n : n + 1] for n in range(6)]
    inputs = x[0]
    normed[0] = (normal(inputs)[0] * (1.0 + row[1]) + row[0]).astype(BF16)
    pieces.wait(0, 4)
    for n in range(3):
        packed[0, :, n * D : (n + 1) * D] = nn(normed[0], dest[n]).astype(BF16)
    size = allowed.shape[1]
    blocks = x.shape[1] // size
    total[...] = jnp.zeros_like(total)

    @pl.loop(0, blocks)
    def _(r):
        rows = pl.ds(pl.multiple_of(r * size, size), size)
        own = packed.at[0, rows]
        attend_rows(
            own.at[:, 0:D],
            own.at[:, D : 2 * D],
            own.at[:, 2 * D : 3 * D],
            total.at[rows],
            allowed[0],
        )

    mixed[0] = total[...].astype(BF16)
    out = nn(mixed[0], dest[3])
    projected[0] = out
    after = x[0] + row[2] * out
    if not cross:
        middle[0] = after
        return
    middle[0] = after
    after_low[0] = after.astype(BF16)
    pieces.wait(4, 2)
    cross_query[0] = nn(after_low[0], dest[4]).astype(BF16)
    total[...] = jnp.zeros_like(total)

    @pl.loop(0, blocks)
    def _(r):
        rows = pl.ds(pl.multiple_of(r * size, size), size)
        attend_rows(
            cross_query.at[0, rows],
            pair.at[0, :, 0:D],
            pair.at[0, :, D : 2 * D],
            total.at[rows],
            None,
        )

    cross_mixed[0] = total[...].astype(BF16)
    middle[0] += nn(cross_mixed[0], dest[5])


def per_video(shape):
    return pl.BlockSpec((1,) + shape[1:], lambda v: (v,) + (0,) * (len(shape) - 1))


def block_call(kernel, name, place, values, weights, outs, scratch, flops):
    any_spec = pl.BlockSpec(memory_space=pl.ANY)
    moved = sum(v.size * v.dtype.itemsize for v in list(values) + list(weights) + list(outs))
    return pl.pallas_call(
        kernel,
        grid=(values[0].shape[0],),
        out_shape=outs,
        in_specs=[pl.BlockSpec(memory_space=pltpu.SMEM)]
        + [per_video(v.shape) for v in values]
        + [any_spec] * len(weights),
        out_specs=[per_video(v.shape) for v in outs],
        scratch_shapes=scratch,
        compiler_params=pltpu.CompilerParams(
            dimension_semantics=("arbitrary",), vmem_limit_bytes=VMEM_LIMIT
        ),
        cost_estimate=pl.CostEstimate(flops=flops, bytes_accessed=moved, transcendentals=0),
        name=name,
    )(place, *values, *weights)


def weight_scratch(count):
    return [pltpu.VMEM((count, D, D), BF16), pltpu.SemaphoreType.DMA((count, 2 * LINES))]


def plan_of(pieces):
    arrays, plan = [], []
    for piece in pieces:
        for array, entry in piece:
            known = [n for n, one in enumerate(arrays) if one is array]
            if not known:
                arrays.append(array)
            plan.append((known[0] if known else len(arrays) - 1, entry))
    return arrays, plan


def attention_forward(place, rows6, x, allowed, pair, pieces):
    arrays, plan = plan_of(pieces)
    cross = pair is not None
    videos, rows, _ = x.shape

    def shape(width, dtype):
        return jax.ShapeDtypeStruct((videos, rows, width), dtype)

    outs = [shape(D, F32), shape(3 * D, BF16), shape(D, F32), shape((4 if cross else 2) * D, BF16)]
    if cross:
        outs += [shape(D, BF16)]
    values = [rows6, x, allowed] + ([pair] if cross else [])
    return block_call(
        lambda *refs: attention_kernel(cross, plan, *refs),
        "attention_forward",
        place,
        values,
        arrays,
        outs,
        weight_scratch(len(pieces)) + [pltpu.VMEM((rows, D), F32)],
        2 * videos * rows * D * (len(pieces) * D + 1024),
    )


def cross_back_kernel(plan, place, grad, pair, query, *refs):
    count = max(ref for ref, _ in plan) + 1
    weights, refs = refs[:count], refs[count:]
    grad_x, rights, grad_pair, dest, sems, grad_mixed, grad_q = refs
    c = jnp.bitwise_and(place[2], 1)
    pieces = Pieces(plan, place, weights, dest, sems, [c, 1 - c])
    pieces.start()
    size = QUERIES
    blocks = grad.shape[1] // size
    grad_query, grad_out = rights.at[:, :, 0:D], rights.at[:, :, D : 2 * D]
    grad_out[0] = grad[0].astype(BF16)
    pieces.wait(0, 2)
    grad_mixed[...] = nt(grad_out[0], dest[1]).astype(BF16)
    grad_q[...] = jnp.zeros_like(grad_q)
    grad_pair[...] = jnp.zeros_like(grad_pair)

    @pl.loop(0, blocks)
    def _(r):
        rows = pl.ds(pl.multiple_of(r * size, size), size)
        attend_rows_back(
            query.at[0, rows],
            pair.at[0, :, 0:D],
            pair.at[0, :, D : 2 * D],
            grad_mixed.at[rows],
            grad_q.at[rows],
            grad_pair.at[0, :, 0:D],
            grad_pair.at[0, :, D : 2 * D],
            None,
        )

    grad_query[0] = grad_q[...].astype(BF16)
    grad_x[0] = grad[0] + nt(grad_query[0], dest[0])


def cross_backward(place, grad, pair, query, pieces):
    arrays, plan = plan_of(pieces)
    videos, rows, _ = grad.shape
    return block_call(
        lambda *refs: cross_back_kernel(plan, *refs),
        "cross_backward",
        place,
        [grad, pair, query],
        arrays,
        [
            jax.ShapeDtypeStruct((videos, rows, D), F32),
            jax.ShapeDtypeStruct((videos, rows, 2 * D), BF16),
            jax.ShapeDtypeStruct(pair.shape, F32),
        ],
        weight_scratch(2) + [pltpu.VMEM((rows, D), BF16), pltpu.VMEM((rows, D), F32)],
        2 * videos * rows * D * (2 * D + 1024),
    )


def attention_back_kernel(plan, place, rows6, x, allowed, packed, projected, grad, *refs):
    count = max(ref for ref, _ in plan) + 1
    weights, refs = refs[:count], refs[count:]
    grad_x, rights, six, dest, sems, grad_mixed, grad_q, grad_k, grad_v = refs
    grad_packed, grad_proj = rights.at[:, :, 0 : 3 * D], rights.at[:, :, 3 * D : 4 * D]
    j = place[2]
    pieces = Pieces(
        plan, place, weights, dest, sems, [jnp.bitwise_xor(j, k) for k in range(4)]
    )
    pieces.start()
    row = [rows6[0, n : n + 1] for n in range(6)]
    size = allowed.shape[1]
    blocks = x.shape[1] // size
    six[0, 2:3] = jnp.sum(grad[0] * projected[0], axis=0, keepdims=True)
    grad_proj[0] = (grad[0] * row[2]).astype(BF16)
    pieces.wait(0, 4)
    grad_mixed[...] = nt(grad_proj[0], dest[3]).astype(BF16)
    for one in (grad_q, grad_k, grad_v):
        one[...] = jnp.zeros_like(one)

    @pl.loop(0, blocks)
    def _(r):
        rows = pl.ds(pl.multiple_of(r * size, size), size)
        own = packed.at[0, rows]
        attend_rows_back(
            own.at[:, 0:D],
            own.at[:, D : 2 * D],
            own.at[:, 2 * D : 3 * D],
            grad_mixed.at[rows],
            grad_q.at[rows],
            grad_k.at[rows],
            grad_v.at[rows],
            allowed[0],
        )

    for n, one in enumerate((grad_q, grad_k, grad_v)):
        grad_packed[0, :, n * D : (n + 1) * D] = one[...].astype(BF16)
    grad_q[...] = nt(grad_packed[0, :, 0:D], dest[0])
    grad_q[...] += nt(grad_packed[0, :, D : 2 * D], dest[1])
    grad_q[...] += nt(grad_packed[0, :, 2 * D : 3 * D], dest[2])
    normed, scale = normal(x[0])
    six[0, 0:1] = jnp.sum(grad_q[...], axis=0, keepdims=True)
    six[0, 1:2] = jnp.sum(grad_q[...] * normed, axis=0, keepdims=True)
    grad_x[0] = grad[0] + normal_back(normed, scale, grad_q[...] * (1.0 + row[1]))


def attention_backward(place, rows6, x, allowed, packed, projected, grad, pieces):
    arrays, plan = plan_of(pieces)
    videos, rows, _ = x.shape
    return block_call(
        lambda *refs: attention_back_kernel(plan, *refs),
        "attention_backward",
        place,
        [rows6, x, allowed, packed, projected, grad],
        arrays,
        [
            jax.ShapeDtypeStruct((videos, rows, D), F32),
            jax.ShapeDtypeStruct((videos, rows, 4 * D), BF16),
            jax.ShapeDtypeStruct((videos, 8, D), F32),
        ],
        weight_scratch(len(pieces))
        + [pltpu.VMEM((rows, D), BF16)]
        + [pltpu.VMEM((rows, D), F32)] * 3,
        2 * videos * rows * D * (len(pieces) * D + 2048),
    )


def mlp_kernel(plan, place, rows6, x, *refs):
    count = max(ref for ref, _ in plan) + 1
    weights, refs = refs[:count], refs[count:]
    hidden, normed, ups, active, lowered, dest, sems = refs
    pieces = Pieces(plan, place, weights, dest, sems, range(8))
    pieces.start()
    row = [rows6[0, n : n + 1] for n in range(6)]
    normed[0] = (normal(x[0])[0] * (1.0 + row[4]) + row[3]).astype(BF16)
    for n in range(4):
        lanes = slice(n * D, (n + 1) * D)
        pieces.wait(n, 1)
        pieces.wait(4 + n, 1)
        up = nn(normed[0], dest[n])
        ups[0, :, lanes] = up
        active[0, :, lanes] = gelu_parts(up)[0].astype(BF16)
        part = nt(active[0, :, lanes], dest[4 + n])
        if n == 0:
            lowered[0] = part
        else:
            lowered[0] += part
    hidden[0] = x[0] + row[5] * lowered[0]


def mlp_forward(place, rows6, x, up, down):
    arrays, plan = plan_of(up + down)
    videos, rows, _ = x.shape

    def shape(width, dtype):
        return jax.ShapeDtypeStruct((videos, rows, width), dtype)

    return block_call(
        lambda *refs: mlp_kernel(plan, *refs),
        "mlp_forward",
        place,
        [rows6, x],
        arrays,
        [shape(D, F32), shape(D, BF16), shape(FF, F32), shape(FF, BF16), shape(D, F32)],
        weight_scratch(8),
        4 * videos * rows * D * FF,
    )


def mlp_back_kernel(plan, place, rows6, x, ups, lowered, grad, *refs):
    count = max(ref for ref, _ in plan) + 1
    weights, refs = refs[:count], refs[count:]
    grad_x, grad_ups, six, dest, sems, total = refs
    pieces = Pieces(plan, place, weights, dest, sems, range(8))
    pieces.start()
    row = [rows6[0, n : n + 1] for n in range(6)]
    six[0, 5:6] = jnp.sum(grad[0] * lowered[0], axis=0, keepdims=True)
    grad_low = (grad[0] * row[5]).astype(BF16)
    for n in range(4):
        lanes = slice(n * D, (n + 1) * D)
        pieces.wait(n, 1)
        pieces.wait(4 + n, 1)
        grad_active = nn(grad_low, dest[4 + n])
        grad_ups[0, :, lanes] = (grad_active * gelu_parts(ups[0, :, lanes])[1]).astype(BF16)
        part = nt(grad_ups[0, :, lanes], dest[n])
        if n == 0:
            total[...] = part
        else:
            total[...] += part
    normed, scale = normal(x[0])
    six[0, 3:4] = jnp.sum(total[...], axis=0, keepdims=True)
    six[0, 4:5] = jnp.sum(total[...] * normed, axis=0, keepdims=True)
    grad_x[0] = grad[0] + normal_back(normed, scale, total[...] * (1.0 + row[4]))


def mlp_backward(place, rows6, x, ups, lowered, grad, up, down):
    arrays, plan = plan_of(up + down)
    videos, rows, _ = x.shape

    def shape(width, dtype):
        return jax.ShapeDtypeStruct((videos, rows, width), dtype)

    return block_call(
        lambda *refs: mlp_back_kernel(plan, *refs),
        "mlp_backward",
        place,
        [rows6, x, ups, lowered, grad],
        arrays,
        [
            shape(D, F32),
            shape(FF, BF16),
            jax.ShapeDtypeStruct((videos, 8, D), F32),
        ],
        weight_scratch(8) + [pltpu.VMEM((rows, D), F32)],
        4 * videos * rows * D * FF,
    )


def outer_kernel(received, lefts_at, rights_at, place, left, right, *refs):
    added, out = refs[:received], refs[received]
    z, y = place[0], place[1]
    total = tn(left[...], right[...])
    for row in range(LINES):
        for column in range(2):
            at = (row * 2 + column) * BLOCK
            block = total[at : at + BLOCK]
            where = (jnp.bitwise_xor(column, y), jnp.bitwise_xor(row, z))
            for one in added:
                block = block + one[0, where[0], where[1]].astype(F32)
            out[0, where[0], where[1]] = block.astype(BF16)


def outer_pieces(place, lefts, rights, which, added=()):
    lefts, rights = lefts.reshape(-1, lefts.shape[-1]), rights.reshape(-1, rights.shape[-1])
    count = len(which)
    rows = lefts.shape[0]
    tables = [
        jnp.stack([jnp.asarray(pick[n], jnp.int32) for pick in which]) for n in range(2)
    ]
    shape = (count, 2, LINES, BLOCK, D)
    piece = pl.BlockSpec((1,) + shape[1:], lambda n, *_: (n, 0, 0, 0, 0))
    return pl.pallas_call(
        lambda *refs: outer_kernel(len(added), *refs),
        grid_spec=pltpu.PrefetchScalarGridSpec(
            num_scalar_prefetch=3,
            grid=(count,),
            in_specs=[
                pl.BlockSpec((rows, D), lambda n, l, r, p: (0, l[n])),
                pl.BlockSpec((rows, D), lambda n, l, r, p: (0, r[n])),
            ]
            + [piece] * len(added),
            out_specs=piece,
        ),
        out_shape=jax.ShapeDtypeStruct(shape, BF16),
        compiler_params=pltpu.CompilerParams(
            dimension_semantics=("arbitrary",), vmem_limit_bytes=VMEM_LIMIT
        ),
        cost_estimate=pl.CostEstimate(
            flops=2 * count * rows * D * D,
            bytes_accessed=2 * count * D * (2 * rows + D * (1 + len(added))),
            transcendentals=0,
        ),
        name="outer_pieces",
    )(*tables, place, lefts, rights, *added)


def optimizer_step(grad, first_old, second_old, master):
    first = BETA_ONE * first_old + (1.0 - BETA_ONE) * grad
    second = BETA_TWO * second_old + (1.0 - BETA_TWO) * grad * grad
    update = (
        first
        / (1.0 - BETA_ONE**STEP)
        / (jnp.sqrt(second / (1.0 - BETA_TWO**STEP)) + ADAM_EPS)
        + DECAY_RATE * master
    )
    return first, second, update


def moments_kernel(ranges, order, scale, *refs):
    grads, refs = refs[: len(ranges)], refs[len(ranges) :]
    first_old, second_old, master, first, second, update, squares, grad = refs
    n = pl.program_id(0)
    for one, pieces in zip(grads, ranges):

        @pl.when((n >= pieces[0]) & (n <= pieces[-1]))
        def _(one=one, pieces=pieces):
            grad[...] = one[0].astype(F32)

    value = grad[...] * scale[0]
    first[...], second[...], step = optimizer_step(
        value, first_old[...], second_old[...], master[...]
    )
    update[...] = step.astype(BF16)
    squares[0, 0:1] = jnp.sum(step * step, axis=0, keepdims=True)
    squares[0, 1:2] = jnp.sum(master[...] * master[...], axis=0, keepdims=True)


def moments(groups, order, scale, first_old, second_old, master):
    rows, width = master.shape
    count = width // D
    column = pl.BlockSpec((rows, D), lambda n, *_: (0, n))
    whole = jax.ShapeDtypeStruct(master.shape, F32)

    def entry(low, high):
        return pl.BlockSpec(
            (1, rows, D), lambda n, order, s: (order[jnp.clip(n, low, high)], 0, 0)
        )

    return pl.pallas_call(
        lambda *refs: moments_kernel([(low, high) for low, high, _ in groups], *refs),
        grid_spec=pltpu.PrefetchScalarGridSpec(
            num_scalar_prefetch=2,
            grid=(count,),
            in_specs=[entry(low, high) for low, high, _ in groups] + [column] * 3,
            out_specs=[column] * 3 + [pl.BlockSpec((1, 2, D), lambda n, *_: (n, 0, 0))],
            scratch_shapes=[pltpu.VMEM((rows, D), F32)],
        ),
        out_shape=[
            whole,
            whole,
            jax.ShapeDtypeStruct(master.shape, BF16),
            jax.ShapeDtypeStruct((count, 2, D), F32),
        ],
        compiler_params=pltpu.CompilerParams(
            dimension_semantics=("arbitrary",), vmem_limit_bytes=VMEM_LIMIT
        ),
        cost_estimate=pl.CostEstimate(
            flops=20 * master.size, bytes_accessed=24 * master.size, transcendentals=0
        ),
        name="moments",
    )(order, scale, *[grads for _, _, grads in groups], first_old, second_old, master)


def row_moments_kernel(scale, grad, first_old, second_old, master, first, second, update, squares):
    grad = grad[...].astype(F32) * scale[0]
    first[...], second[...], step = optimizer_step(
        grad, first_old[...], second_old[...], master[...]
    )
    update[...] = step.astype(BF16)

    @pl.when(pl.program_id(0) == 0)
    def _():
        squares[...] = jnp.zeros_like(squares)

    squares[0:1] += jnp.sum(step * step, axis=0, keepdims=True)
    squares[1:2] += jnp.sum(master[...] * master[...], axis=0, keepdims=True)


def row_step(rows):
    return 16 if rows % 16 == 0 else rows


def row_moments(scale, grads, first_old, second_old, master):
    rows, width = master.shape
    step = row_step(rows)
    block = pl.BlockSpec((step, width), lambda n, *_: (n, 0))
    whole = jax.ShapeDtypeStruct(master.shape, F32)
    return pl.pallas_call(
        row_moments_kernel,
        grid_spec=pltpu.PrefetchScalarGridSpec(
            num_scalar_prefetch=1,
            grid=(rows // step,),
            in_specs=[block] * 4,
            out_specs=[block] * 3 + [pl.BlockSpec((2, width), lambda n, *_: (0, 0))],
        ),
        out_shape=[
            whole,
            whole,
            jax.ShapeDtypeStruct(master.shape, BF16),
            jax.ShapeDtypeStruct((2, width), F32),
        ],
        compiler_params=pltpu.CompilerParams(
            dimension_semantics=("arbitrary",), vmem_limit_bytes=VMEM_LIMIT
        ),
        cost_estimate=pl.CostEstimate(
            flops=20 * master.size, bytes_accessed=24 * master.size, transcendentals=0
        ),
        name="row_moments",
    )(scale, grads, first_old, second_old, master)


def apply_kernel(trust, master, update, new, copy):
    value = master[...] - trust[...] * update[...].astype(F32)
    new[...] = value
    copy[...] = value.astype(BF16)


def apply_pieces_kernel(trust, master, update, new, copy):
    value = master[...] - trust[pl.program_id(0)] * update[...].astype(F32)
    new[...] = value
    copy[...] = value.astype(BF16)


def apply_update(trust, master, update):
    rows, width = master.shape
    step = row_step(rows)
    outs = [
        jax.ShapeDtypeStruct(master.shape, F32),
        jax.ShapeDtypeStruct(master.shape, BF16),
    ]
    params = pltpu.CompilerParams(
        dimension_semantics=("arbitrary",), vmem_limit_bytes=VMEM_LIMIT
    )
    cost = pl.CostEstimate(
        flops=4 * master.size, bytes_accessed=12 * master.size, transcendentals=0
    )
    if trust.ndim == 1:
        block = pl.BlockSpec((rows, D), lambda n, *_: (0, n))
        return pl.pallas_call(
            apply_pieces_kernel,
            grid_spec=pltpu.PrefetchScalarGridSpec(
                num_scalar_prefetch=1,
                grid=(width // D,),
                in_specs=[block, block],
                out_specs=[block, block],
            ),
            out_shape=outs,
            compiler_params=params,
            cost_estimate=cost,
            name="apply_pieces",
        )(trust, master, update)
    block = pl.BlockSpec((step, width), lambda n: (n, 0))
    return pl.pallas_call(
        apply_kernel,
        grid=(rows // step,),
        in_specs=[pl.BlockSpec((1, width), lambda n: (0, 0)), block, block],
        out_specs=[block, block],
        out_shape=outs,
        compiler_params=params,
        cost_estimate=cost,
        name="apply_update",
    )(trust, master, update)


def own_piece(shard, index):
    return lax.dynamic_slice(shard, (0, index * D), (shard.shape[0], D)).astype(BF16)


def pick_kernel(count, spatial_at, temporal_at, spatial, temporal, out):
    n = pl.program_id(0)

    @pl.when(n < count)
    def _():
        out[0] = spatial[...].astype(BF16)

    @pl.when(n >= count)
    def _():
        out[0] = temporal[...].astype(BF16)


def own_pieces(spatial, temporal, spatial_at, temporal_at):
    rows = spatial.shape[0]
    count, total = len(spatial_at), len(spatial_at) + len(temporal_at)
    spatial_at = spatial_at + spatial_at[-1:] * len(temporal_at)
    temporal_at = temporal_at[:1] * count + temporal_at
    tables = [
        jnp.stack([jnp.asarray(one, jnp.int32) for one in at]) for at in (spatial_at, temporal_at)
    ]
    return pl.pallas_call(
        lambda *refs: pick_kernel(count, *refs),
        grid_spec=pltpu.PrefetchScalarGridSpec(
            num_scalar_prefetch=2,
            grid=(total,),
            in_specs=[
                pl.BlockSpec((rows, D), lambda n, s, t: (0, s[n])),
                pl.BlockSpec((rows, D), lambda n, s, t: (0, t[n])),
            ],
            out_specs=pl.BlockSpec((1, rows, D), lambda n, *_: (n, 0, 0)),
        ),
        out_shape=jax.ShapeDtypeStruct((total, rows, D), BF16),
        compiler_params=pltpu.CompilerParams(
            dimension_semantics=("arbitrary",), vmem_limit_bytes=VMEM_LIMIT
        ),
        name="own_pieces",
    )(*tables, spatial, temporal)


def gathered_piece(shard, index):
    rows = lax.all_gather(own_piece(shard, index), "fsdp", axis=0, tiled=True)
    blocks = jnp.swapaxes(rows.reshape(LINES, 2, BLOCK, D), 0, 1)
    return ((blocks, 0), (blocks, 1))


def plus(kept, received):
    return (kept.astype(F32) + received.astype(F32)).astype(BF16)


def scatter_whole(pieces):
    whole = jnp.swapaxes(pieces, 1, 2).reshape(pieces.shape[0], D, D)
    return lax.psum_scatter(whole, "fsdp", scatter_dimension=1, tiled=True)


class Scatter:
    def __init__(self, pieces):
        self.pieces = pieces
        self.explicit = few("fsdp")

    def along_y(self, after=()):
        if not self.explicit:
            return self.pieces
        self.half = swap(gate(self.pieces[:, 1], after), "fsdp", 1)
        return self.half

    def along_z(self, after=()):
        if not self.explicit:
            return self.pieces
        self.half = plus(self.pieces[:, 0], self.half)
        self.quarter = swap(gate(self.half[:, 2:], after), "fsdp", 4)
        return self.quarter

    def end(self, after=()):
        if not self.explicit:
            self.rows = scatter_whole(self.pieces)
            return self.rows
        quarter = plus(self.half[:, :2], self.quarter)
        self.rows = plus(quarter[:, 0], swap(gate(quarter[:, 1], after), "fsdp", 2))
        return self.rows


def share(total):
    total = plus(total, swap(total[::-1], "frame", 2))
    return total, swap(total, "frame", 1)


def exchange_parts(parts):
    sent = swap(jnp.stack([parts[1], parts[3]]), "frame", 1)
    crossed = swap(jnp.stack([parts[2], sent[1]]), "frame", 2)
    return [parts[0], sent[0], crossed[0], crossed[1]]


def to_tokens(values):
    j, size = lax.axis_index("frame"), lax.axis_size("frame")
    videos, frames, tokens, width = values.shape
    part = tokens // (size * frames)
    halves = tokens // (size * part)
    cut = values.reshape(videos, frames, size, halves, part, width)
    parts = exchange_parts(
        [lax.dynamic_index_in_dim(cut, j ^ k, 2, False) for k in range(size)]
    )
    received = [jnp.swapaxes(one, 1, 2) for one in parts]
    return jnp.stack(received, axis=2).reshape(videos, halves * tokens, width)


def from_tokens(values, frames):
    j, size = lax.axis_index("frame"), lax.axis_size("frame")
    videos, rows, width = values.shape
    tokens_part = rows // (size * frames)
    tokens = tokens_part * size
    part = tokens // (size * frames)
    halves = tokens_part // part
    cut = values.reshape(videos, halves, size, frames, part, width)
    whole = jnp.zeros((videos, frames, size, halves, part, width), values.dtype)
    for k, block in enumerate(exchange_parts([cut[:, :, k] for k in range(size)])):
        block = jnp.swapaxes(block, 1, 2)[:, :, None]
        whole = lax.dynamic_update_slice_in_dim(whole, block, j ^ k, axis=2)
    return whole.reshape(videos, frames, tokens, width)


def local(
    latents,
    added_noise,
    text_states,
    timesteps,
    token_counts,
    frame_counts,
    w_shared,
    w_spatial,
    w_temporal,
    shift_tables,
    m_shared,
    m_spatial,
    m_temporal,
    m_tables,
    v_shared,
    v_spatial,
    v_temporal,
    v_tables,
):
    i, j = lax.axis_index("fsdp"), lax.axis_index("frame")
    c = j % 2
    n_fsdp, n_frame = lax.axis_size("fsdp"), lax.axis_size("frame")
    rows_own = w_shared.shape[0]
    frames = latents.shape[2]
    frames_all = frames * n_frame
    videos = latents.shape[0] * latents.shape[1]
    tokens = latents.shape[3]
    texts = text_states.shape[2]

    explicit = few("fsdp")
    if explicit:
        mine = own_pieces(
            w_spatial,
            w_temporal,
            [j, jnp.where(c == 0, 4, 7), 8 + j, 12 + j],
            [j, 4 + j, 4 + (j ^ 2), 8 + j, 8 + (j ^ 2)],
        )
        first, rest = mine[:1], mine[1:]
        first_near = jnp.stack([first, swap(first, "fsdp", 2)], axis=1)

    shared_parts = split_columns(w_shared, shared_widths())
    if explicit:
        shared_parts = gate(shared_parts, [first])
    patch_own, time_one, caption_w, time_two, mod_w, final_own = shared_parts
    time_one, time_two, mod_w = [one.astype(BF16) for one in (time_one, time_two, mod_w)]
    pair_w = w_spatial[:, 5 * D : 7 * D].astype(BF16)
    steps_own = timesteps.reshape(videos)
    steps_two = jnp.concatenate([steps_own // 32, steps_own % 32]).astype(BF16)[:, None]
    small = jnp.concatenate(
        [
            patch_own.T.astype(BF16),
            final_own.T.astype(BF16),
            shift_tables.T.astype(BF16),
            jnp.broadcast_to(steps_two, (2 * videos, rows_own)),
        ]
    )
    small = jnp.pad(small, ((0, -small.shape[0] % 16), (0, 0)))
    small = collect(small, "fsdp")
    at = 2 * PCH + 14
    steps_all = small[:, at : at + 2 * videos, 0].astype(F32)
    steps_all = steps_all[:, :videos] * 32.0 + steps_all[:, videos:]
    small = jnp.swapaxes(to_relative(small, "fsdp"), 0, 1).reshape(small.shape[1], D)
    patch_w, final_w = small[:PCH], small[PCH : 2 * PCH]
    tables = small[2 * PCH : at].astype(F32)

    cond_index = jnp.where(few("fsdp"), i, 0)
    place = jnp.stack([cond_index // 2, cond_index % 2, j]).astype(jnp.int32)

    step_float = timesteps.reshape(videos).astype(F32)
    token_count = token_counts.reshape(videos)
    alpha_bar = jnp.cos((step_float / 1000.0 + 0.008) / 1.008 * (math.pi / 2)) ** 2
    snr_value = alpha_bar / (1.0 - alpha_bar)
    loss_weight = jnp.minimum(snr_value, SNR_GAMMA) / snr_value

    half_count = FREQ // 2
    frequency = jnp.exp(-math.log(10000.0) * jnp.arange(half_count, dtype=F32) / half_count)
    angles = steps_all.reshape(-1)[:, None] * frequency[None, :]
    features = jnp.concatenate([jnp.cos(angles), jnp.sin(angles)], axis=-1).astype(BF16)
    hidden_pre = dot_t(features, time_one)
    hidden_act = jax.nn.silu(hidden_pre).astype(BF16)
    embedding_all = sum_relative(dot(hidden_act, time_two).reshape(n_fsdp, videos, D), "fsdp")
    embedding = embedding_all[0]
    embedding_part = lax.dynamic_slice(
        embedding_all.reshape(-1, D), (0, i * rows_own), (n_fsdp * videos, rows_own)
    )
    embed_act = jax.nn.silu(embedding_part).astype(BF16)
    mod_half = dot(embed_act, lax.dynamic_slice(mod_w, (0, c * 3 * D), (rows_own, 3 * D)))
    mod_half = deliver(mod_half.reshape(n_fsdp, videos, 3 * D), "fsdp")
    mod_other = swap(mod_half, "frame", 1)
    modulation = jnp.concatenate(
        [jnp.where(c == 0, mod_half, mod_other), jnp.where(c == 0, mod_other, mod_half)], axis=1
    ).reshape(videos, 6, D)
    six_spatial = modulation + tables[None, 0:6]
    six_temporal = modulation + tables[None, 6:12]
    final_rows = embedding[:, None, :] + tables[None, 12:14]

    text_part = TXT_D // n_frame
    text_own = text_states.reshape(videos * texts, TXT_D)
    text_own = lax.dynamic_slice(text_own, (0, j * text_part), (videos * texts, text_part))
    text_all = collect(text_own, "fsdp").reshape(-1, text_part)
    caption_part = lax.dynamic_slice(caption_w, (0, j * text_part), (rows_own, text_part))
    caption_part = caption_part.astype(BF16)
    caption_pre = sum_over_frame_low(dot_t(text_all, caption_part))
    caption = gelu_tanh(caption_pre).astype(BF16)
    pair_part = 2 * D // n_frame
    pair_w_part = lax.dynamic_slice(pair_w, (0, j * pair_part), (rows_own, pair_part))
    pair = dot(caption, pair_w_part).astype(BF16).reshape(n_fsdp, videos * texts, pair_part)
    pair = collect(deliver(pair, "fsdp").astype(BF16), "frame")
    pair = jnp.swapaxes(to_relative(pair, "frame"), 0, 1).reshape(videos, texts, 2 * D)

    target = to_tokens(added_noise.reshape(videos, frames, tokens, PCH)).astype(F32)

    if explicit:

        def with_far(near, after):
            return jnp.concatenate([near, swap(gate(near, after), "fsdp", 4)], axis=1)

        def y(lines, after):
            return swap(gate(lines, after), "fsdp", 1)

        def x(lines, after):
            return swap(gate(lines, after), "frame", 2)

        def core(lines, after):
            return swap(gate(lines, after), "frame", 1)

        def joined(*arrays):
            return jnp.concatenate(arrays)

        done = [first_near]
        la = with_far(first_near, done)
        rest_near = jnp.stack([rest, swap(gate(rest, done), "fsdp", 2)], axis=1)
        done = [la, rest_near, text_all]
        lbc = with_far(rest_near[0:2], done)
        ya, xla = y(la, done), x(la, done)
        done = [lbc, ya, xla, caption_pre]
        lde = with_far(rest_near[2:4], done)
        ybc, x1 = y(lbc, done), x(joined(ya, lbc[1:]), done)
        k1 = core(joined(la, xla), done)
        done = [lde, ybc, x1, k1, pair, modulation]
        lf = with_far(rest_near[4:6], done)
        yde, x2 = y(lde, done), x(joined(ybc[1:], lde), done)
        k2 = core(joined(ya, x1[:1], lbc, ybc), done)
        done = [lf, yde, x2, k2]
        lg = with_far(rest_near[6:8], done)
        yf, xyde = y(lf, done), x(yde, done)
        k3 = core(joined(x1[1:], lde, x2, yde), done)
        spatial_attn = [
            ((la, 0), (ya, 0)),
            ((k1, 0), (k2, 0)),
            ((xla, 0), (x1, 0)),
            ((k1, 1), (k2, 1)),
        ]
        cross_attn = [((lbc, 0), (ybc, 0)), ((k2, 2), (k2, 4))]
    else:
        done = []
        spatial_attn = [gathered_piece(w_spatial, j ^ k) for k in range(4)]
        cross_attn = [
            gathered_piece(w_spatial, jnp.where(c == n, 4, 7)) for n in range(2)
        ]
        spatial_up, spatial_down = [
            [gathered_piece(w_spatial, base + (j ^ k)) for k in range(4)] for base in (8, 12)
        ]
        temporal_attn, temporal_up, temporal_down = [
            [gathered_piece(w_temporal, base + (j ^ k)) for k in range(4)] for base in (0, 4, 8)
        ]

    noise_own = added_noise.reshape(videos, frames * tokens, PCH)
    clean = latents.reshape(videos, frames * tokens, PCH).astype(F32)
    noisy = (
        jnp.sqrt(alpha_bar)[:, None, None] * clean
        + jnp.sqrt(1.0 - alpha_bar)[:, None, None] * noise_own.astype(F32)
    ).astype(BF16)
    start = gate(dot(noisy, patch_w), done)
    key_valid = (jnp.arange(tokens)[None, :] < token_count[:, None]).astype(F32)
    spatial_allowed = jnp.broadcast_to(key_valid[:, :, None], (videos, tokens, tokens))
    middle1, packed1, projected1, lefts1, cross_query = attention_forward(
        place, six_spatial, start, spatial_allowed, pair, spatial_attn + cross_attn
    )
    if explicit:
        done = [lg, yf, xyde, k3, middle1, fence(middle1)]
        yg = y(lg, done)
        k4 = core(xyde, done)
        k5 = core(joined(lf, yf), [k4])
        spatial_up = [
            ((lbc, 1), (ybc, 1)),
            ((k2, 3), (k2, 5)),
            ((x1, 1), (x2, 0)),
            ((k3, 0), (k3, 3)),
        ]
        spatial_down, temporal_attn = [
            [
                ((lde, n), (yde, n)),
                ((k3, 1 + n), (k3, 6 + n)),
                ((x2, 1 + n), (xyde, n)),
                ((k3, 4 + n), (k4, n)),
            ]
            for n in range(2)
        ]
        middle1 = gate(middle1, done)
    hidden1, normed1, ups1, active1, lowered1 = mlp_forward(
        place, six_spatial, middle1, spatial_up, spatial_down
    )

    hidden = to_tokens(hidden1.reshape(videos, frames, tokens, D))
    rows = hidden.shape[1]
    part = tokens // frames_all
    clip_ends = jnp.cumsum(frame_counts.reshape(videos, -1), axis=-1)
    block_row = jnp.arange(tokens, dtype=jnp.int32)
    frame_at = ((block_row // (frames * part)) ^ j) * frames + block_row // part % frames
    segment = jnp.sum(
        (frame_at[None, :, None] >= clip_ends[:, None, :]).astype(jnp.int32), axis=-1
    )
    same_token = (block_row % part)[:, None] == (block_row % part)[None, :]
    same = same_token[None] & (segment[:, :, None] == segment[:, None, :])
    temporal_allowed = same.astype(F32)
    token_at = (
        j * (tokens // n_frame)
        + jnp.arange(rows, dtype=jnp.int32) // tokens * part
        + jnp.arange(rows, dtype=jnp.int32) % part
    )
    if explicit:
        done = [yg, k5, hidden]
        k6 = core(joined(lg, yg), done)
        temporal_up, temporal_down = [
            [((l, 0), (b, 0)), ((k, 0), (k, 2)), ((l, 1), (b, 1)), ((k, 1), (k, 3))]
            for l, b, k in ((lf, yf, k5), (lg, yg, k6))
        ]
        hidden = gate(hidden, done)
    middle2, packed2, projected2, lefts2 = attention_forward(
        place, six_temporal, hidden, temporal_allowed, None, temporal_attn
    )
    hidden2, normed2, ups2, active2, lowered2 = mlp_forward(
        place, six_temporal, middle2, temporal_up, temporal_down
    )

    shift_final = final_rows[:, 0][:, None, :]
    scale_final = final_rows[:, 1][:, None, :]
    normed_final = modulate(hidden2, shift_final, scale_final).astype(BF16)
    predicted = dot_t(normed_final, final_w)
    pred_error = predicted - target
    keep_weight = (token_at[None, :] < token_count[:, None]).astype(F32) * loss_weight[:, None]
    keep_weight = keep_weight[:, :, None]
    loss_part = jnp.sum(keep_weight * pred_error * pred_error) / PCH
    weight_part = jnp.sum(loss_weight * token_count.astype(F32)) * frames_all

    grad_pred = (keep_weight * pred_error * (2.0 / PCH)).astype(BF16)
    grad_final_w = outer(grad_pred, normed_final)
    grad_hidden2, grad_shift_final, grad_scale_final = modulate_back(
        hidden2, shift_final, scale_final, dot(grad_pred, final_w)
    )
    slots = [(0, k) for k in range(4)]
    low2 = (grad_hidden2 * six_temporal[:, 5][:, None, :]).astype(BF16)

    def pieces_of(lefts, rights, which, after=(), added=()):
        return outer_pieces(place, gate(lefts, after), rights, which, added)

    other1 = pieces_of(low2, active2, [slots[3], slots[1]])
    core1 = swap(other1, "frame", 1)
    grad_middle2, grad_ups2, six_mlp2 = mlp_backward(
        place,
        six_temporal,
        middle2,
        ups2,
        lowered2,
        gate(grad_hidden2, [other1]),
        temporal_up,
        temporal_down,
    )
    done = [core1, grad_middle2, fence(grad_middle2)]
    second1 = pieces_of(low2, active2, [slots[2]], done, (core1[:1],))
    x1 = swap(second1, "frame", 2)
    other2 = pieces_of(normed2, grad_ups2, [slots[1], slots[3]], [second1])
    core2 = swap(other2, "frame", 1)
    grad_hidden, rights2, six_attn2 = attention_backward(
        place,
        six_temporal,
        hidden,
        temporal_allowed,
        packed2,
        projected2,
        gate(grad_middle2, [other2]),
        temporal_attn,
    )
    done = [core2, grad_hidden, fence(grad_hidden)]
    sum2 = Scatter(pieces_of(normed2, grad_ups2, [slots[0], slots[2]], done, (core2,)))
    y2 = sum2.along_y()
    grad_hidden1 = from_tokens(gate(grad_hidden, [sum2.pieces]), frames)
    grad_hidden1 = grad_hidden1.reshape(videos, frames * tokens, D)
    which2 = [((j ^ k) // 3, j ^ k) for k in range(4)]
    other3 = pieces_of(lefts2, rights2, [which2[3], which2[1]], [sum2.pieces])
    core3 = swap(other3, "frame", 1)
    sum1 = Scatter(pieces_of(low2, active2, [slots[0]], [other3], (core1[1:], x1)))
    y1 = sum1.along_y()
    second3 = pieces_of(lefts2, rights2, [which2[2]], [sum1.pieces], (core3[:1],))
    done = [grad_hidden1, sum1.pieces, second3, y2]
    x3 = swap(gate(second3, done), "frame", 2)
    low1 = (gate(grad_hidden1, done) * six_spatial[:, 5][:, None, :]).astype(BF16)
    other4 = pieces_of(low1, active1, [slots[3], slots[1]])
    core4 = swap(other4, "frame", 1)
    z2 = sum2.along_z(done)
    grad_middle1, grad_ups1, six_mlp1 = mlp_backward(
        place,
        six_spatial,
        middle1,
        ups1,
        lowered1,
        gate(grad_hidden1, [other4]),
        spatial_up,
        spatial_down,
    )
    done = [core4, grad_middle1, fence(grad_middle1), y1]
    second4 = pieces_of(low1, active1, [slots[2]], done, (core4[:1],))
    x4 = swap(second4, "frame", 2)
    z1 = sum1.along_z(done)
    other5 = pieces_of(normed1, grad_ups1, [slots[1], slots[3]], [second4])
    core5 = swap(other5, "frame", 1)
    grad_after1, rights7, grad_pair = cross_backward(
        place, gate(grad_middle1, [other5]), pair, cross_query, cross_attn
    )
    sum3 = Scatter(pieces_of(lefts2, rights2, [which2[0]], [grad_after1], (core3[1:], x3)))
    y3 = sum3.along_y()
    rows2 = sum2.end([sum3.pieces])
    done = [core5, sum3.pieces, z1, z2]
    sum5 = Scatter(pieces_of(normed1, grad_ups1, [slots[0], slots[2]], done, (core5,)))
    y5 = sum5.along_y()
    other7 = pieces_of(lefts1, rights7, [(3 - c, 1 - c)], [sum5.pieces])
    core7 = swap(other7, "frame", 1)
    grad_pair = grad_pair.astype(BF16).reshape(videos * texts, n_frame, pair_part)
    grad_pair = to_relative(jnp.swapaxes(grad_pair, 0, 1), "frame")
    grad_pair = deliver(grad_pair, "frame").astype(BF16)
    rows1 = sum1.end([other7])
    grad_start, rights1, six_attn1 = attention_backward(
        place,
        six_spatial,
        start,
        spatial_allowed,
        packed1,
        projected1,
        gate(grad_after1, [other7]),
        spatial_attn,
    )
    sum4 = Scatter(pieces_of(low1, active1, [slots[0]], [grad_start], (core4[1:], x4)))
    done = [grad_start, core7, y3, sum4.pieces, grad_pair, rows1, rows2]

    along_pair = collect_along(gate(grad_pair, done))
    six_s, six_t = [
        jnp.concatenate([attn[:, 0:3], mlp[:, 3:6]], axis=1)
        for attn, mlp in ((gate(six_attn1, done), six_mlp1), (six_attn2, six_mlp2))
    ]
    grad_final = jnp.stack([grad_shift_final, grad_scale_final], axis=1)
    grad_patch_w = outer(noisy, grad_start.astype(BF16))
    cond = jnp.concatenate(
        [
            grad_patch_w,
            grad_final_w,
            jnp.sum(jnp.concatenate([six_s, six_t, grad_final], axis=1), axis=0),
            jnp.concatenate([six_s + six_t, grad_final], axis=1).reshape(-1, D),
        ]
    )
    cond = sum_over(cond, "frame")

    y4, z3 = sum4.along_y([along_pair]), sum3.along_z([along_pair])
    which1 = [((j ^ k) // 3, j ^ k) for k in range(4)]
    other6 = pieces_of(lefts1, rights1, [which1[1], which1[3]], done)
    core6 = swap(other6, "frame", 1)
    sum7 = Scatter(pieces_of(lefts1, rights7, [(2 + c, c)], [other6], (core7,)))
    y7 = sum7.along_y()
    pair6 = pieces_of(lefts1, rights1, [which1[0], which1[2]], [sum7.pieces], (core6,))
    sum6, sum8 = Scatter(pair6[:1]), Scatter(pair6[1:])
    done = [pair6, y4, z3, y5, along_pair, cond]
    grad_pair = collect_beside(gate(along_pair, done)).reshape(-1, pair_part)
    small_grad = jnp.swapaxes(cond[: 2 * PCH + 14].reshape(-1, n_fsdp, rows_own), 0, 1)
    small_grad = deliver_beside(gate(to_relative(small_grad, "fsdp"), done))
    along_cond = collect_along(
        gate(cond[2 * PCH + 14 :].astype(BF16).reshape(videos, 8, D), done)
    )
    first_sent = [grad_pair, small_grad, along_cond]
    y6 = sum6.along_y(first_sent)
    y8 = sum8.along_y([y7] + first_sent)
    z4, z5 = sum4.along_z(first_sent), sum5.along_z(first_sent)
    rows3 = sum3.end(done)
    done = [y7, z4, z5, rows3] + first_sent
    pair_w_grad = outer(caption, gate(grad_pair, done))
    grad_caption = sum_over_frame_low(dot_t(grad_pair, pair_w_part))
    small_grad = deliver_along(gate(small_grad, done)).T
    cond = collect_beside(gate(along_cond, done)).reshape(n_fsdp * videos, 8, D)
    first_sent = [cond, small_grad]
    z7 = sum7.along_z(first_sent)
    z6 = sum6.along_z([y6] + first_sent)
    rows4, rows5 = sum4.end(done), sum5.end(done)
    done = [y8, z7, rows4, rows5, grad_caption] + first_sent
    grad_caption = jax.vjp(gelu_tanh, caption_pre)[1](gate(grad_caption, done))[0].astype(BF16)
    both = jnp.concatenate([outer(grad_caption, text_all), pair_w_grad], axis=1).astype(BF16)
    both = collect(both, "frame")
    grad_mod = gate(cond, done)[:, :6].reshape(-1, 6 * D)
    mod_grad = outer(embed_act, grad_mod)
    final_part = lax.dynamic_slice(
        cond[:, 6].astype(F32) + cond[:, 7].astype(F32), (0, i * rows_own), embedding_part.shape
    )
    grad_embed = (
        jax.vjp(jax.nn.silu, embedding_part)[1](dot_t(grad_mod, mod_w))[0] + final_part
    ).astype(BF16)
    along_embed = collect_along(grad_embed.reshape(n_fsdp, videos, rows_own))
    z8 = sum8.along_z([along_embed, y8])
    rows7 = sum7.end([along_embed])
    quads = jnp.stack([rows1, rows3, rows4], axis=1)
    slots_two = jnp.stack([rows2, rows5], axis=1)
    crossed = swap(jnp.concatenate([slots_two[1], slots_two[0], quads[0]]), "frame", 2)
    totals = jnp.concatenate([plus(slots_two.reshape(4, rows_own, D), crossed[:4]), quads[0], crossed[4:]])
    done = [z6, z8, rows7, along_embed, totals, both]
    received = collect_beside(gate(along_embed, done))
    rows6, rows8 = sum6.end([received]), sum8.end([received])
    totals_other = swap(gate(totals, done), "frame", 1)
    crossed7 = swap(gate(rows7, done), "frame", 2)
    done = [rows6, rows8, totals_other, crossed7, received]
    last = jnp.concatenate([rows6, rows8])
    crossed = swap(gate(last[::-1], done), "frame", 2)
    last = jnp.concatenate([plus(last, crossed), plus(rows7, crossed7)])
    last_other = swap(last, "frame", 1)

    def in_order(total, other):
        return jnp.stack([total, other], axis=1).reshape((-1,) + total.shape[1:])

    up_grads2, up_grads1, down_grads2, attn_grads2, down_grads1 = [
        in_order(jnp.stack([totals[m], totals[n]]), jnp.stack([totals_other[m], totals_other[n]]))
        for m, n in ((0, 2), (1, 3), (4, 7), (5, 8), (6, 9))
    ]
    attn_grads1 = in_order(last[:2], last_other[:2])
    cross_grads = jnp.concatenate([last[2:], last_other[2:]])
    both = to_relative(both, "frame")
    caption_grad, pair_w_grad = [
        jnp.swapaxes(one, 0, 1).reshape(rows_own, -1)
        for one in (both[:, :, :text_part], both[:, :, text_part:])
    ]
    step = np.arange(n_fsdp)
    grad_embed = received[step[:, None], step[:, None] ^ step[None, :]]
    grad_embed = jnp.transpose(to_relative(grad_embed, "fsdp"), (1, 2, 0, 3)).reshape(-1, D)
    time_two_grad = outer(hidden_act, grad_embed)
    grad_hidden = dot_t(grad_embed, time_two)
    grad_hidden = jax.vjp(jax.nn.silu, hidden_pre)[1](grad_hidden)[0].astype(BF16)
    time_one_grad = outer(grad_hidden, features)
    shared_grads = jnp.concatenate(
        [
            small_grad[:, :PCH].astype(BF16),
            time_one_grad.astype(BF16),
            caption_grad,
            time_two_grad.astype(BF16),
            mod_grad.astype(BF16),
            small_grad[:, PCH : 2 * PCH].astype(BF16),
        ],
        axis=1,
    )

    pair_pieces = jnp.stack([pair_w_grad[:, :D], pair_w_grad[:, D:]])
    tables_grad = small_grad[:, 2 * PCH :]
    relative = jnp.arange(4, dtype=jnp.int32) ^ j
    spatial_order = jnp.concatenate(
        [
            relative,
            jnp.stack([c, 0 * c, 1 + 0 * c, 1 - c]).astype(jnp.int32),
            relative,
            relative,
        ]
    )
    temporal_order = jnp.concatenate([relative, relative, relative])
    spatial_groups = [
        (0, 3, attn_grads1),
        (4, 4, cross_grads),
        (5, 6, pair_pieces),
        (7, 7, cross_grads),
        (8, 11, up_grads1),
        (12, 15, down_grads1),
    ]
    temporal_groups = [(0, 3, attn_grads2), (4, 7, up_grads2), (8, 11, down_grads2)]

    def squares(values, axes=None):
        values = values.astype(F32)
        return jnp.sum(values * values, axis=axes)

    def group_squares(groups, order):
        return jnp.concatenate(
            [
                squares(grads, (1, 2))[order[low : high + 1]]
                for low, high, grads in groups
            ]
        )

    def rows_of(widths, first):
        which = np.repeat(np.arange(len(widths)) + first, widths)
        return jnp.asarray(which)[None, :] == jnp.arange(18)[:, None]

    shared_rows = rows_of(shared_widths(), 0)
    spatial_rows = rows_of([width // D for width in spatial_widths()], 6)
    temporal_rows = rows_of([width // D for width in temporal_widths()], 13)

    def matrix_sums(shared, spatial, temporal, table):
        totals = jnp.where(jnp.arange(18) == 17, table, 0.0)
        for marks, values in (
            (shared_rows, shared),
            (spatial_rows, spatial),
            (temporal_rows, temporal),
        ):
            totals = totals + jnp.sum(jnp.where(marks, values[None, :], 0.0), axis=1)
        return totals

    def spread(marks, values):
        return jnp.sum(jnp.where(marks, values[:, None], 0.0), axis=0)

    grad_part_sq = matrix_sums(
        squares(shared_grads, 0),
        group_squares(spatial_groups, spatial_order),
        group_squares(temporal_groups, temporal_order),
        squares(tables_grad),
    )
    loss_all = sum_over(loss_part[None], "frame")
    numbers = sum_over(jnp.concatenate([grad_part_sq, loss_all, weight_part[None]]), "fsdp")
    grad_sq, loss_sum, weight_total = numbers[:18], numbers[18], numbers[19]
    grad_norm = jnp.sqrt(jnp.sum(grad_sq)) / weight_total
    factor = CLIP_NORM / jnp.maximum(grad_norm, CLIP_NORM)
    grad_scale = factor / weight_total
    scale = grad_scale[None]
    shared_new = row_moments(scale, shared_grads, m_shared, v_shared, w_shared)
    spatial_new = moments(spatial_groups, spatial_order, scale, m_spatial, v_spatial, w_spatial)
    temporal_new = moments(
        temporal_groups, temporal_order, scale, m_temporal, v_temporal, w_temporal
    )
    tables_new = optimizer_step(tables_grad * grad_scale, m_tables, v_tables, shift_tables)
    spatial_sq = jnp.sum(spatial_new[3], axis=2)
    temporal_sq = jnp.sum(temporal_new[3], axis=2)
    numbers = [
        matrix_sums(shared_new[3][n], spatial_sq[:, n], temporal_sq[:, n], squares(table))
        for n, table in enumerate((tables_new[2], shift_tables))
    ]
    numbers = sum_over(jnp.concatenate(numbers), "fsdp")
    update_sq, weight_sq = numbers[:18], numbers[18:]
    trust = LEARN_RATE * jnp.sqrt(weight_sq) / jnp.sqrt(update_sq)
    new_shared, copy_shared = apply_update(
        spread(shared_rows, trust)[None], w_shared, shared_new[2]
    )
    new_spatial, copy_spatial = apply_update(
        spread(spatial_rows, trust), w_spatial, spatial_new[2]
    )
    new_temporal, copy_temporal = apply_update(
        spread(temporal_rows, trust), w_temporal, temporal_new[2]
    )
    new_tables = shift_tables - trust[17] * tables_new[2]
    return (
        loss_sum,
        weight_total,
        grad_norm,
        jnp.stack([jnp.sqrt(weight_sq), jnp.sqrt(update_sq)]),
        jnp.sqrt(grad_sq) * grad_scale,
        new_shared,
        new_spatial,
        new_temporal,
        new_tables,
        shared_new[0],
        spatial_new[0],
        temporal_new[0],
        tables_new[0],
        shared_new[1],
        spatial_new[1],
        temporal_new[1],
        tables_new[1],
        copy_shared,
        copy_spatial,
        copy_temporal,
        new_tables.astype(BF16),
    )


def solution(mesh):
    rows = P("fsdp", None)
    return jax.shard_map(
        local,
        mesh=mesh,
        in_specs=(
            P(None, "fsdp", "frame", None, None),
            P(None, "fsdp", "frame", None, None),
            P(None, "fsdp", None, None),
            P(None, "fsdp"),
            P(None, "fsdp"),
            P(None, "fsdp", None),
        )
        + (rows,) * 12,
        out_specs=(P(),) * 5 + (rows,) * 16,
        check_vma=False,
    )
```

```python
import math

import jax
import jax.numpy as jnp
import numpy as np
from jax import lax
from jax.experimental import pallas as pl
from jax.experimental.pallas import tpu as pltpu
from jax.sharding import PartitionSpec as P

D = 1152
HEADS = 16
HEAD_DIM = 72
FF = 4608
TXT_D = 4096
FREQ = 256
PCH = 16
STEP = 10

CLIP_NORM = 0.01
LEARN_RATE = 0.3
BETA_ONE = 0.9
BETA_TWO = 0.999
ADAM_EPS = 1e-06
DECAY_RATE = 0.01
SNR_GAMMA = 5.0
NORM_EPS = 1e-06

F32 = jnp.float32
BF16 = jnp.bfloat16


def few(axis):
    return lax.axis_size(axis) <= 8


def swap(values, axis, mask):
    return lax.ppermute(values, axis, [(n, n ^ mask) for n in range(lax.axis_size(axis))])


def order_of(axis):
    return jnp.arange(lax.axis_size(axis), dtype=jnp.int32) ^ lax.axis_index(axis)


def to_relative(stacked, axis):
    return jnp.take(stacked, order_of(axis), axis=0)


def masks(axis):
    return [m for m in (2, 4, 1) if m < lax.axis_size(axis)] if axis == "fsdp" else [1, 2]


def gate(values, after):
    return lax.optimization_barrier((values, after))[0]


def sum_over(values, axis):
    if not few(axis):
        return lax.psum(values, axis)
    for mask in masks(axis):
        values = values + swap(values, axis, mask)
    return values


def sum_over_frame_low(values):
    for mask in (1, 2):
        low = values.astype(BF16)
        values = low.astype(F32) + swap(low, "frame", mask).astype(F32)
    return values


def collect(values, axis):
    if not few(axis):
        return to_relative(lax.all_gather(values, axis, axis=0), axis)
    blocks = values[None]
    for mask in masks(axis):
        blocks = jnp.concatenate([blocks, swap(blocks, axis, mask)])
    if axis == "frame":
        return blocks
    size = lax.axis_size(axis)
    return jnp.swapaxes(blocks.reshape((2, size // 2) + values.shape), 0, 1).reshape(blocks.shape)


class Collect:
    def __init__(self, values):
        self.values = values
        self.explicit = few("fsdp")
        if self.explicit:
            size = lax.axis_size("fsdp")
            self.sent = [swap(values, "fsdp", mask) for mask in range(2, size, 2)]

    def beside(self, after=()):
        if self.explicit:
            self.values = jnp.stack([self.values] + gate(self.sent, after))
            self.sent = swap(self.values, "fsdp", 1)

    def all(self, after=()):
        if not self.explicit:
            return collect(self.values, "fsdp")
        both = jnp.stack([self.values, gate(self.sent, after)], axis=1)
        return both.reshape((-1,) + self.values.shape[1:])


class Deliver:
    def __init__(self, blocks):
        self.blocks = blocks
        self.explicit = few("fsdp")
        if self.explicit:
            self.pairs = blocks.reshape((-1, 2) + blocks.shape[1:])
            self.sent = [
                swap(self.pairs[k], "fsdp", 2 * k) for k in range(1, self.pairs.shape[0])
            ]

    def beside(self, after=()):
        if self.explicit:
            sent = gate(self.sent, after)
            self.half = self.pairs[0]
            for one in sent:
                self.half = self.half + one
            self.sent = swap(self.half[1], "fsdp", 1)

    def total(self, after=()):
        if not self.explicit:
            return deliver(self.blocks, "fsdp")
        return self.half[0] + gate(self.sent, after)


def fence(values):
    flat = values.reshape(-1, values.shape[-1])
    return swap(flat[:8, :128], "frame", 1)


def deliver(blocks, axis):
    size = lax.axis_size(axis)
    if not few(axis):
        return lax.psum_scatter(to_relative(blocks, axis), axis, scatter_dimension=0).astype(F32)
    kind = blocks.dtype
    held = list(range(size))
    for mask in masks(axis)[::-1]:
        keep = [k for k in held if not k & mask]
        low = blocks.astype(kind)
        received = swap(jnp.stack([low[held.index(k ^ mask)] for k in keep]), axis, mask)
        blocks = jnp.stack([blocks[held.index(k)] for k in keep]).astype(F32)
        blocks = blocks + received.astype(F32)
        held = keep
    return blocks[0]


def sum_relative(blocks, axis):
    size = lax.axis_size(axis)
    if not few(axis):
        return to_relative(lax.psum(to_relative(blocks, axis), axis), axis)
    for mask in masks(axis):
        received = swap(blocks, axis, mask)
        blocks = blocks + jnp.stack([received[k ^ mask] for k in range(size)])
    return blocks


def layer_norm(values):
    centered = values - jnp.mean(values, axis=-1, keepdims=True)
    return centered * lax.rsqrt(jnp.mean(centered * centered, axis=-1, keepdims=True) + NORM_EPS)


def modulate(residual, shift_by, scale_by):
    return layer_norm(residual) * (1.0 + scale_by) + shift_by


def gelu_tanh(values):
    return jax.nn.gelu(values, approximate=True)


def shared_widths():
    return (PCH, FREQ, TXT_D, D, 6 * D, PCH)


def spatial_widths():
    return (3 * D, D, D, 2 * D, D, FF, FF)


def temporal_widths():
    return (3 * D, D, FF, FF)


def split_columns(weight, widths):
    pieces = []
    offset = 0
    for column_count in widths:
        pieces.append(weight[:, offset : offset + column_count])
        offset += column_count
    return pieces


def dot(left, right):
    return lax.dot_general(
        left,
        right,
        (((left.ndim - 1,), (0,)), ((), ())),
        preferred_element_type=F32,
    )


def dot_t(left, right):
    return lax.dot_general(
        left,
        right,
        (((left.ndim - 1,), (1,)), ((), ())),
        preferred_element_type=F32,
    )


def outer(left, right):
    return lax.dot_general(
        left.reshape(-1, left.shape[-1]),
        right.reshape(-1, right.shape[-1]),
        (((0,), (0,)), ((), ())),
        preferred_element_type=F32,
    )


def modulate_back(residual, shift_by, scale_by, grad):
    grad_residual, grad_shift, grad_scale = jax.vjp(modulate, residual, shift_by, scale_by)[1](grad)
    return grad_residual, grad_shift[:, 0], grad_scale[:, 0]


LINES = 4
QUERIES = 128
BLOCK = D // (2 * LINES)
VMEM_LIMIT = 58 * 2**20
SHORT = pl.CostEstimate(flops=1000, bytes_accessed=1000, transcendentals=0)
SCALE = 1.0 / math.sqrt(HEAD_DIM)


def nn(left, right):
    return lax.dot_general(left, right, (((1,), (0,)), ((), ())), preferred_element_type=F32)


def nt(left, right):
    return lax.dot_general(left, right, (((1,), (1,)), ((), ())), preferred_element_type=F32)


def tn(left, right):
    return lax.dot_general(left, right, (((0,), (0,)), ((), ())), preferred_element_type=F32)


class Pieces:
    def __init__(self, plan, place, refs, dest, sems, indices):
        z, y = place[0], place[1]
        self.copies = []
        for n, index in enumerate(indices):
            for k in range(LINES):
                for m, column in enumerate((y, 1 - y)):
                    ref, entry = plan[2 * n + m]
                    row = pl.multiple_of((jnp.bitwise_xor(z, k) * 2 + column) * BLOCK, BLOCK)
                    self.copies.append(
                        pltpu.make_async_copy(
                            refs[ref].at[entry, k],
                            dest.at[index, pl.ds(row, BLOCK)],
                            sems.at[n, 2 * k + m],
                        )
                    )

    def start(self):
        @pl.when(pl.program_id(0) == 0)
        def _():
            for copy in self.copies:
                copy.start()

    def wait(self, first, count):
        @pl.when(pl.program_id(0) == 0)
        def _():
            for copy in self.copies[2 * LINES * first : 2 * LINES * (first + count)]:
                copy.wait()


def windows():
    for head in range(HEADS):
        first = head * HEAD_DIM
        start = first // 128 * 128
        yield first - start, start, (256 if first - start + HEAD_DIM > 128 else 128)


def head_mask(offset, width):
    lane = lax.broadcasted_iota(jnp.int32, (1, width), 1)
    return jnp.where((lane >= offset) & (lane < offset + HEAD_DIM), 1.0, 0.0).astype(BF16)


def soft_columns(scores, allowed):
    scores = scores * SCALE
    if allowed is not None:
        scores = jnp.where(allowed > 0.5, scores, -1e30)
    grown = jnp.exp(scores - jnp.max(scores, axis=0, keepdims=True))
    return grown / jnp.sum(grown, axis=0, keepdims=True)


def attend_rows(query, key, value, out, allowed):
    for offset, start, width in windows():
        mask = head_mask(offset, width)
        lanes = slice(start, start + width)
        soft = soft_columns(nt(key[:, lanes], query[:, lanes] * mask), allowed)
        out[:, lanes] += tn(soft.astype(BF16), value[:, lanes] * mask)


def attend_rows_back(query, key, value, grad, grad_query, grad_key, grad_value, allowed):
    for offset, start, width in windows():
        mask = head_mask(offset, width)
        lanes = slice(start, start + width)
        query_head = query[:, lanes] * mask
        key_head = key[:, lanes] * mask
        grad_head = grad[:, lanes] * mask
        soft = soft_columns(nt(key_head, query_head), allowed)
        grad_soft = nt(value[:, lanes], grad_head)
        grad_value[:, lanes] += nn(soft.astype(BF16), grad_head)
        grad_scores = soft * (grad_soft - jnp.sum(soft * grad_soft, axis=0, keepdims=True))
        grad_scores = (grad_scores * SCALE).astype(BF16)
        grad_key[:, lanes] += nn(grad_scores, query_head)
        grad_query[:, lanes] += tn(grad_scores, key_head)


def normal(values):
    centered = values - jnp.mean(values, axis=-1, keepdims=True)
    scale = lax.rsqrt(jnp.mean(centered * centered, axis=-1, keepdims=True) + NORM_EPS)
    return centered * scale, scale


def normal_back(normed, scale, grad):
    return scale * (
        grad
        - jnp.mean(grad, axis=-1, keepdims=True)
        - normed * jnp.mean(grad * normed, axis=-1, keepdims=True)
    )


def gelu_parts(values):
    root = math.sqrt(2.0 / math.pi)
    square = values * values
    bent = jnp.tanh(root * (values + 0.044715 * (values * square)))
    half = 0.5 * (1.0 + bent)
    slope = half + 0.5 * values * (1.0 - bent * bent) * (root * (1.0 + 3 * 0.044715 * square))
    return values * half, slope


def attention_kernel(cross, plan, place, rows6, x, allowed, *refs):
    if cross:
        pair, refs = refs[0], refs[1:]
    count = max(ref for ref, _ in plan) + 1
    weights, refs = refs[:count], refs[count:]
    if cross:
        (middle, packed, projected, lefts, cross_query) = refs[:5]
        refs = refs[5:]
        after_low, cross_mixed = lefts.at[:, :, 2 * D : 3 * D], lefts.at[:, :, 3 * D : 4 * D]
    else:
        (middle, packed, projected, lefts) = refs[:4]
        refs = refs[4:]
    normed, mixed = lefts.at[:, :, 0:D], lefts.at[:, :, D : 2 * D]
    dest, sems, total = refs
    j = place[2]
    indices = [jnp.bitwise_xor(j, k) for k in range(4)]
    if cross:
        c = jnp.bitwise_and(j, 1)
        indices += [4 + c, 5 - c]
    pieces = Pieces(plan, place, weights, dest, sems, indices)
    pieces.start()
    row = [rows6[0, n : n + 1] for n in range(6)]
    inputs = x[0]
    normed[0] = (normal(inputs)[0] * (1.0 + row[1]) + row[0]).astype(BF16)
    pieces.wait(0, 4)
    for n in range(3):
        packed[0, :, n * D : (n + 1) * D] = nn(normed[0], dest[n]).astype(BF16)
    size = allowed.shape[1]
    blocks = x.shape[1] // size
    total[...] = jnp.zeros_like(total)

    @pl.loop(0, blocks)
    def _(r):
        rows = pl.ds(pl.multiple_of(r * size, size), size)
        own = packed.at[0, rows]
        attend_rows(
            own.at[:, 0:D],
            own.at[:, D : 2 * D],
            own.at[:, 2 * D : 3 * D],
            total.at[rows],
            allowed[0],
        )

    mixed[0] = total[...].astype(BF16)
    out = nn(mixed[0], dest[3])
    projected[0] = out
    after = x[0] + row[2] * out
    if not cross:
        middle[0] = after
        return
    middle[0] = after
    after_low[0] = after.astype(BF16)
    pieces.wait(4, 2)
    cross_query[0] = nn(after_low[0], dest[4]).astype(BF16)
    total[...] = jnp.zeros_like(total)

    @pl.loop(0, blocks)
    def _(r):
        rows = pl.ds(pl.multiple_of(r * size, size), size)
        attend_rows(
            cross_query.at[0, rows],
            pair.at[0, :, 0:D],
            pair.at[0, :, D : 2 * D],
            total.at[rows],
            None,
        )

    cross_mixed[0] = total[...].astype(BF16)
    middle[0] += nn(cross_mixed[0], dest[5])


def per_video(shape):
    return pl.BlockSpec((1,) + shape[1:], lambda v: (v,) + (0,) * (len(shape) - 1))


def block_call(kernel, name, place, values, weights, outs, scratch, flops):
    any_spec = pl.BlockSpec(memory_space=pl.ANY)
    moved = sum(v.size * v.dtype.itemsize for v in list(values) + list(weights) + list(outs))
    return pl.pallas_call(
        kernel,
        grid=(values[0].shape[0],),
        out_shape=outs,
        in_specs=[pl.BlockSpec(memory_space=pltpu.SMEM)]
        + [per_video(v.shape) for v in values]
        + [any_spec] * len(weights),
        out_specs=[per_video(v.shape) for v in outs],
        scratch_shapes=scratch,
        compiler_params=pltpu.CompilerParams(
            dimension_semantics=("arbitrary",), vmem_limit_bytes=VMEM_LIMIT
        ),
        cost_estimate=SHORT,
        name=name,
    )(place, *values, *weights)


def weight_scratch(count):
    return [pltpu.VMEM((count, D, D), BF16), pltpu.SemaphoreType.DMA((count, 2 * LINES))]


def plan_of(pieces):
    arrays, plan = [], []
    for piece in pieces:
        for array, entry in piece:
            known = [n for n, one in enumerate(arrays) if one is array]
            if not known:
                arrays.append(array)
            plan.append((known[0] if known else len(arrays) - 1, entry))
    return arrays, plan


def attention_forward(place, rows6, x, allowed, pair, pieces):
    arrays, plan = plan_of(pieces)
    cross = pair is not None
    videos, rows, _ = x.shape

    def shape(width, dtype):
        return jax.ShapeDtypeStruct((videos, rows, width), dtype)

    outs = [shape(D, F32), shape(3 * D, BF16), shape(D, F32), shape((4 if cross else 2) * D, BF16)]
    if cross:
        outs += [shape(D, BF16)]
    values = [rows6, x, allowed] + ([pair] if cross else [])
    return block_call(
        lambda *refs: attention_kernel(cross, plan, *refs),
        "attention_forward",
        place,
        values,
        arrays,
        outs,
        weight_scratch(len(pieces)) + [pltpu.VMEM((rows, D), F32)],
        2 * videos * rows * D * (len(pieces) * D + 1024),
    )


def cross_back_kernel(plan, place, grad, pair, query, *refs):
    count = max(ref for ref, _ in plan) + 1
    weights, refs = refs[:count], refs[count:]
    grad_x, rights, grad_pair, dest, sems, grad_mixed, grad_q = refs
    c = jnp.bitwise_and(place[2], 1)
    pieces = Pieces(plan, place, weights, dest, sems, [c, 1 - c])
    pieces.start()
    size = QUERIES
    blocks = grad.shape[1] // size
    grad_query, grad_out = rights.at[:, :, 0:D], rights.at[:, :, D : 2 * D]
    grad_out[0] = grad[0].astype(BF16)
    pieces.wait(0, 2)
    grad_mixed[...] = nt(grad_out[0], dest[1]).astype(BF16)
    grad_q[...] = jnp.zeros_like(grad_q)
    grad_pair[...] = jnp.zeros_like(grad_pair)

    @pl.loop(0, blocks)
    def _(r):
        rows = pl.ds(pl.multiple_of(r * size, size), size)
        attend_rows_back(
            query.at[0, rows],
            pair.at[0, :, 0:D],
            pair.at[0, :, D : 2 * D],
            grad_mixed.at[rows],
            grad_q.at[rows],
            grad_pair.at[0, :, 0:D],
            grad_pair.at[0, :, D : 2 * D],
            None,
        )

    grad_query[0] = grad_q[...].astype(BF16)
    grad_x[0] = grad[0] + nt(grad_query[0], dest[0])


def cross_backward(place, grad, pair, query, pieces):
    arrays, plan = plan_of(pieces)
    videos, rows, _ = grad.shape
    return block_call(
        lambda *refs: cross_back_kernel(plan, *refs),
        "cross_backward",
        place,
        [grad, pair, query],
        arrays,
        [
            jax.ShapeDtypeStruct((videos, rows, D), F32),
            jax.ShapeDtypeStruct((videos, rows, 2 * D), BF16),
            jax.ShapeDtypeStruct(pair.shape, F32),
        ],
        weight_scratch(2) + [pltpu.VMEM((rows, D), BF16), pltpu.VMEM((rows, D), F32)],
        2 * videos * rows * D * (2 * D + 1024),
    )


def attention_back_kernel(plan, place, rows6, x, allowed, packed, projected, grad, *refs):
    count = max(ref for ref, _ in plan) + 1
    weights, refs = refs[:count], refs[count:]
    grad_x, rights, six, dest, sems, grad_mixed, grad_q, grad_k, grad_v = refs
    grad_packed, grad_proj = rights.at[:, :, 0 : 3 * D], rights.at[:, :, 3 * D : 4 * D]
    j = place[2]
    pieces = Pieces(
        plan, place, weights, dest, sems, [jnp.bitwise_xor(j, k) for k in range(4)]
    )
    pieces.start()
    row = [rows6[0, n : n + 1] for n in range(6)]
    size = allowed.shape[1]
    blocks = x.shape[1] // size
    six[0, 2:3] = jnp.sum(grad[0] * projected[0], axis=0, keepdims=True)
    grad_proj[0] = (grad[0] * row[2]).astype(BF16)
    pieces.wait(0, 4)
    grad_mixed[...] = nt(grad_proj[0], dest[3]).astype(BF16)
    for one in (grad_q, grad_k, grad_v):
        one[...] = jnp.zeros_like(one)

    @pl.loop(0, blocks)
    def _(r):
        rows = pl.ds(pl.multiple_of(r * size, size), size)
        own = packed.at[0, rows]
        attend_rows_back(
            own.at[:, 0:D],
            own.at[:, D : 2 * D],
            own.at[:, 2 * D : 3 * D],
            grad_mixed.at[rows],
            grad_q.at[rows],
            grad_k.at[rows],
            grad_v.at[rows],
            allowed[0],
        )

    for n, one in enumerate((grad_q, grad_k, grad_v)):
        grad_packed[0, :, n * D : (n + 1) * D] = one[...].astype(BF16)
    grad_q[...] = nt(grad_packed[0, :, 0:D], dest[0])
    grad_q[...] += nt(grad_packed[0, :, D : 2 * D], dest[1])
    grad_q[...] += nt(grad_packed[0, :, 2 * D : 3 * D], dest[2])
    normed, scale = normal(x[0])
    six[0, 0:1] = jnp.sum(grad_q[...], axis=0, keepdims=True)
    six[0, 1:2] = jnp.sum(grad_q[...] * normed, axis=0, keepdims=True)
    grad_x[0] = grad[0] + normal_back(normed, scale, grad_q[...] * (1.0 + row[1]))


def attention_backward(place, rows6, x, allowed, packed, projected, grad, pieces):
    arrays, plan = plan_of(pieces)
    videos, rows, _ = x.shape
    return block_call(
        lambda *refs: attention_back_kernel(plan, *refs),
        "attention_backward",
        place,
        [rows6, x, allowed, packed, projected, grad],
        arrays,
        [
            jax.ShapeDtypeStruct((videos, rows, D), F32),
            jax.ShapeDtypeStruct((videos, rows, 4 * D), BF16),
            jax.ShapeDtypeStruct((videos, 8, D), F32),
        ],
        weight_scratch(len(pieces))
        + [pltpu.VMEM((rows, D), BF16)]
        + [pltpu.VMEM((rows, D), F32)] * 3,
        2 * videos * rows * D * (len(pieces) * D + 2048),
    )


def mlp_kernel(plan, place, rows6, x, *refs):
    count = max(ref for ref, _ in plan) + 1
    weights, refs = refs[:count], refs[count:]
    hidden, normed, ups, active, lowered, dest, sems = refs
    pieces = Pieces(plan, place, weights, dest, sems, range(8))
    pieces.start()
    row = [rows6[0, n : n + 1] for n in range(6)]
    normed[0] = (normal(x[0])[0] * (1.0 + row[4]) + row[3]).astype(BF16)
    for n in range(4):
        lanes = slice(n * D, (n + 1) * D)
        pieces.wait(n, 1)
        pieces.wait(4 + n, 1)
        up = nn(normed[0], dest[n])
        ups[0, :, lanes] = up
        active[0, :, lanes] = gelu_parts(up)[0].astype(BF16)
        part = nt(active[0, :, lanes], dest[4 + n])
        if n == 0:
            lowered[0] = part
        else:
            lowered[0] += part
    hidden[0] = x[0] + row[5] * lowered[0]


def mlp_forward(place, rows6, x, up, down):
    arrays, plan = plan_of(up + down)
    videos, rows, _ = x.shape

    def shape(width, dtype):
        return jax.ShapeDtypeStruct((videos, rows, width), dtype)

    return block_call(
        lambda *refs: mlp_kernel(plan, *refs),
        "mlp_forward",
        place,
        [rows6, x],
        arrays,
        [shape(D, F32), shape(D, BF16), shape(FF, F32), shape(FF, BF16), shape(D, F32)],
        weight_scratch(8),
        4 * videos * rows * D * FF,
    )


def mlp_back_kernel(plan, place, rows6, x, ups, lowered, grad, *refs):
    count = max(ref for ref, _ in plan) + 1
    weights, refs = refs[:count], refs[count:]
    grad_x, grad_ups, six, dest, sems, total = refs
    pieces = Pieces(plan, place, weights, dest, sems, range(8))
    pieces.start()
    row = [rows6[0, n : n + 1] for n in range(6)]
    six[0, 5:6] = jnp.sum(grad[0] * lowered[0], axis=0, keepdims=True)
    grad_low = (grad[0] * row[5]).astype(BF16)
    for n in range(4):
        lanes = slice(n * D, (n + 1) * D)
        pieces.wait(n, 1)
        pieces.wait(4 + n, 1)
        grad_active = nn(grad_low, dest[4 + n])
        grad_ups[0, :, lanes] = (grad_active * gelu_parts(ups[0, :, lanes])[1]).astype(BF16)
        part = nt(grad_ups[0, :, lanes], dest[n])
        if n == 0:
            total[...] = part
        else:
            total[...] += part
    normed, scale = normal(x[0])
    six[0, 3:4] = jnp.sum(total[...], axis=0, keepdims=True)
    six[0, 4:5] = jnp.sum(total[...] * normed, axis=0, keepdims=True)
    grad_x[0] = grad[0] + normal_back(normed, scale, total[...] * (1.0 + row[4]))


def mlp_backward(place, rows6, x, ups, lowered, grad, up, down):
    arrays, plan = plan_of(up + down)
    videos, rows, _ = x.shape

    def shape(width, dtype):
        return jax.ShapeDtypeStruct((videos, rows, width), dtype)

    return block_call(
        lambda *refs: mlp_back_kernel(plan, *refs),
        "mlp_backward",
        place,
        [rows6, x, ups, lowered, grad],
        arrays,
        [
            shape(D, F32),
            shape(FF, BF16),
            jax.ShapeDtypeStruct((videos, 8, D), F32),
        ],
        weight_scratch(8) + [pltpu.VMEM((rows, D), F32)],
        4 * videos * rows * D * FF,
    )


def outer_kernel(received, split, lefts_at, rights_at, place, left, right, *refs):
    added, outs = refs[:received], refs[received:]
    z, y = place[0], place[1]
    total = tn(left[...], right[...])

    def store(own):
        for row in range(LINES):
            for column in range(2):
                at = (row * 2 + column) * BLOCK
                block = total[at : at + BLOCK]
                beside, along = column ^ own, jnp.bitwise_xor(row, z)
                for one in added:
                    block = block + one[0, beside, along].astype(F32)
                if split:
                    outs[beside][0, along] = block.astype(BF16)
                else:
                    outs[0][0, beside, along] = block.astype(BF16)

    for own in range(2):
        pl.when(y == own)(lambda own=own: store(own))


def outer_pieces(place, lefts, rights, which, added=(), split=False):
    lefts, rights = lefts.reshape(-1, lefts.shape[-1]), rights.reshape(-1, rights.shape[-1])
    count = len(which)
    rows = lefts.shape[0]
    tables = [
        jnp.stack([jnp.asarray(pick[n], jnp.int32) for pick in which]) for n in range(2)
    ]
    shape = (count, 2, LINES, BLOCK, D)
    piece = pl.BlockSpec((1,) + shape[1:], lambda n, *_: (n, 0, 0, 0, 0))
    half = (count, LINES, BLOCK, D)
    half_piece = pl.BlockSpec((1,) + half[1:], lambda n, *_: (n, 0, 0, 0))
    return pl.pallas_call(
        lambda *refs: outer_kernel(len(added), split, *refs),
        grid_spec=pltpu.PrefetchScalarGridSpec(
            num_scalar_prefetch=3,
            grid=(count,),
            in_specs=[
                pl.BlockSpec((rows, D), lambda n, l, r, p: (0, l[n])),
                pl.BlockSpec((rows, D), lambda n, l, r, p: (0, r[n])),
            ]
            + [piece] * len(added),
            out_specs=[half_piece] * 2 if split else piece,
        ),
        out_shape=[jax.ShapeDtypeStruct(half, BF16)] * 2
        if split
        else jax.ShapeDtypeStruct(shape, BF16),
        compiler_params=pltpu.CompilerParams(
            dimension_semantics=("arbitrary",), vmem_limit_bytes=VMEM_LIMIT
        ),
        cost_estimate=SHORT,
        name="outer_pieces",
    )(*tables, place, lefts, rights, *added)


def optimizer_step(grad, first_old, second_old, master):
    first = BETA_ONE * first_old + (1.0 - BETA_ONE) * grad
    second = BETA_TWO * second_old + (1.0 - BETA_TWO) * grad * grad
    update = (
        (first * (1.0 / (1.0 - BETA_ONE**STEP)))
        / (jnp.sqrt(second * (1.0 / (1.0 - BETA_TWO**STEP))) + ADAM_EPS)
        + DECAY_RATE * master
    )
    return first, second, update


def moments_kernel(arrays, source, entry, scale, *refs):
    grads, refs = refs[:arrays], refs[arrays:]
    first_old, second_old, master, first, second, update, squares, grad = refs
    n = pl.program_id(0)
    for number, one in enumerate(grads):

        @pl.when(source[n] == number)
        def _(one=one):
            grad[...] = one[0].astype(F32)

    value = grad[...] * scale[0]
    first[...], second[...], step = optimizer_step(
        value, first_old[...], second_old[...], master[...]
    )
    update[...] = step.astype(BF16)
    squares[0, 0:1] = jnp.sum(step * step, axis=0, keepdims=True)
    squares[0, 1:2] = jnp.sum(master[...] * master[...], axis=0, keepdims=True)


def moments(arrays, source, entry, scale, first_old, second_old, master):
    rows, width = master.shape
    count = width // D
    column = pl.BlockSpec((rows, D), lambda n, *_: (0, n))
    whole = jax.ShapeDtypeStruct(master.shape, F32)

    def block(number):
        return pl.BlockSpec(
            (1, rows, D),
            lambda n, source, entry, _: (jnp.where(source[n] == number, entry[n], 0), 0, 0),
        )

    return pl.pallas_call(
        lambda *refs: moments_kernel(len(arrays), *refs),
        grid_spec=pltpu.PrefetchScalarGridSpec(
            num_scalar_prefetch=3,
            grid=(count,),
            in_specs=[block(number) for number in range(len(arrays))] + [column] * 3,
            out_specs=[column] * 3 + [pl.BlockSpec((1, 2, D), lambda n, *_: (n, 0, 0))],
            scratch_shapes=[pltpu.VMEM((rows, D), F32)],
        ),
        out_shape=[
            whole,
            whole,
            jax.ShapeDtypeStruct(master.shape, BF16),
            jax.ShapeDtypeStruct((count, 2, D), F32),
        ],
        compiler_params=pltpu.CompilerParams(
            dimension_semantics=("arbitrary",), vmem_limit_bytes=VMEM_LIMIT
        ),
        cost_estimate=SHORT,
        name="moments",
    )(source, entry, scale, *arrays, first_old, second_old, master)


def row_moments_kernel(scale, grad, first_old, second_old, master, first, second, update, squares):
    grad = grad[...].astype(F32) * scale[0]
    first[...], second[...], step = optimizer_step(
        grad, first_old[...], second_old[...], master[...]
    )
    update[...] = step.astype(BF16)

    @pl.when(pl.program_id(0) == 0)
    def _():
        squares[...] = jnp.zeros_like(squares)

    squares[0:1] += jnp.sum(step * step, axis=0, keepdims=True)
    squares[1:2] += jnp.sum(master[...] * master[...], axis=0, keepdims=True)


def row_step(rows):
    return 16 if rows % 16 == 0 else rows


def row_moments(scale, grads, first_old, second_old, master):
    rows, width = master.shape
    step = row_step(rows)
    block = pl.BlockSpec((step, width), lambda n, *_: (n, 0))
    whole = jax.ShapeDtypeStruct(master.shape, F32)
    return pl.pallas_call(
        row_moments_kernel,
        grid_spec=pltpu.PrefetchScalarGridSpec(
            num_scalar_prefetch=1,
            grid=(rows // step,),
            in_specs=[block] * 4,
            out_specs=[block] * 3 + [pl.BlockSpec((2, width), lambda n, *_: (0, 0))],
        ),
        out_shape=[
            whole,
            whole,
            jax.ShapeDtypeStruct(master.shape, BF16),
            jax.ShapeDtypeStruct((2, width), F32),
        ],
        compiler_params=pltpu.CompilerParams(
            dimension_semantics=("arbitrary",), vmem_limit_bytes=VMEM_LIMIT
        ),
        cost_estimate=SHORT,
        name="row_moments",
    )(scale, grads, first_old, second_old, master)


def apply_kernel(trust, master, update, new, copy):
    value = master[...] - trust[...] * update[...].astype(F32)
    new[...] = value
    copy[...] = value.astype(BF16)


def apply_pieces_kernel(trust, master, update, new, copy):
    value = master[...] - trust[pl.program_id(0)] * update[...].astype(F32)
    new[...] = value
    copy[...] = value.astype(BF16)


def apply_update(trust, master, update):
    rows, width = master.shape
    step = row_step(rows)
    outs = [
        jax.ShapeDtypeStruct(master.shape, F32),
        jax.ShapeDtypeStruct(master.shape, BF16),
    ]
    params = pltpu.CompilerParams(
        dimension_semantics=("arbitrary",), vmem_limit_bytes=VMEM_LIMIT
    )
    if trust.ndim == 1:
        block = pl.BlockSpec((rows, D), lambda n, *_: (0, n))
        return pl.pallas_call(
            apply_pieces_kernel,
            grid_spec=pltpu.PrefetchScalarGridSpec(
                num_scalar_prefetch=1,
                grid=(width // D,),
                in_specs=[block, block],
                out_specs=[block, block],
            ),
            out_shape=outs,
            compiler_params=params,
            cost_estimate=SHORT,
            name="apply_pieces",
        )(trust, master, update)
    block = pl.BlockSpec((step, width), lambda n: (n, 0))
    return pl.pallas_call(
        apply_kernel,
        grid=(rows // step,),
        in_specs=[pl.BlockSpec((1, width), lambda n: (0, 0)), block, block],
        out_specs=[block, block],
        out_shape=outs,
        compiler_params=params,
        cost_estimate=SHORT,
        name="apply_update",
    )(trust, master, update)


def own_piece(shard, index):
    return lax.dynamic_slice(shard, (0, index * D), (shard.shape[0], D)).astype(BF16)


def pick_kernel(count, spatial_at, temporal_at, spatial, temporal, out):
    n = pl.program_id(0)

    @pl.when(n < count)
    def _():
        out[0] = spatial[...].astype(BF16)

    @pl.when(n >= count)
    def _():
        out[0] = temporal[...].astype(BF16)


def own_pieces(spatial, temporal, spatial_at, temporal_at):
    rows = spatial.shape[0]
    count, total = len(spatial_at), len(spatial_at) + len(temporal_at)
    spatial_at = spatial_at + spatial_at[-1:] * len(temporal_at)
    temporal_at = temporal_at[:1] * count + temporal_at
    tables = [
        jnp.stack([jnp.asarray(one, jnp.int32) for one in at]) for at in (spatial_at, temporal_at)
    ]
    return pl.pallas_call(
        lambda *refs: pick_kernel(count, *refs),
        grid_spec=pltpu.PrefetchScalarGridSpec(
            num_scalar_prefetch=2,
            grid=(total,),
            in_specs=[
                pl.BlockSpec((rows, D), lambda n, s, t: (0, s[n])),
                pl.BlockSpec((rows, D), lambda n, s, t: (0, t[n])),
            ],
            out_specs=pl.BlockSpec((1, rows, D), lambda n, *_: (n, 0, 0)),
        ),
        out_shape=jax.ShapeDtypeStruct((total, rows, D), BF16),
        compiler_params=pltpu.CompilerParams(
            dimension_semantics=("arbitrary",), vmem_limit_bytes=VMEM_LIMIT
        ),
        name="own_pieces",
    )(*tables, spatial, temporal)


def gathered_piece(shard, index):
    rows = lax.all_gather(own_piece(shard, index), "fsdp", axis=0, tiled=True)
    blocks = jnp.swapaxes(rows.reshape(LINES, 2, BLOCK, D), 0, 1)
    return ((blocks, 0), (blocks, 1))


def plus(kept, received):
    return (kept.astype(F32) + received.astype(F32)).astype(BF16)


def scatter_whole(keep, send):
    whole = jnp.stack([keep, send], axis=2).reshape(keep.shape[0], D, D)
    return lax.psum_scatter(whole, "fsdp", scatter_dimension=1, tiled=True)


class Scatter:
    def __init__(self, pieces):
        self.pieces, self.sent = pieces
        self.explicit = few("fsdp")

    def along_y(self, after=()):
        self.sent = gate(self.sent, after)
        if self.explicit:
            self.sent = swap(self.sent, "fsdp", 1)

    def along_z(self, after=()):
        if not self.explicit:
            return self.pieces
        half = plus(gate(self.pieces, after), self.sent)
        self.half, self.sent = half, swap(half[:, 2:], "fsdp", 4)
        return half

    def end_z(self, after=()):
        if not self.explicit:
            return self.pieces
        quarter = plus(gate(self.half[:, :2], after), self.sent)
        self.half, self.sent = quarter, swap(quarter[:, 1], "fsdp", 2)
        return quarter

    def rows(self, after=()):
        if not self.explicit:
            return scatter_whole(self.pieces, self.sent)
        return plus(gate(self.half[:, 0], after), self.sent)


def exchange_parts(parts, between=(), after=()):
    sent = gate(swap(jnp.stack([parts[1], parts[3]]), "frame", 1), between)
    crossed = gate(swap(jnp.stack([parts[2], sent[1]]), "frame", 2), after)
    return [parts[0], sent[0], crossed[0], crossed[1]]


def to_tokens(values, between=()):
    j, size = lax.axis_index("frame"), lax.axis_size("frame")
    videos, frames, tokens, width = values.shape
    part = tokens // (size * frames)
    halves = tokens // (size * part)
    cut = values.reshape(videos, frames, size, halves, part, width)
    parts = exchange_parts(
        [lax.dynamic_index_in_dim(cut, j ^ k, 2, False) for k in range(size)], between
    )
    received = [jnp.swapaxes(one, 1, 2) for one in parts]
    return jnp.stack(received, axis=2).reshape(videos, halves * tokens, width)


def from_tokens(values, frames, between=(), after=()):
    j, size = lax.axis_index("frame"), lax.axis_size("frame")
    videos, rows, width = values.shape
    tokens_part = rows // (size * frames)
    tokens = tokens_part * size
    part = tokens // (size * frames)
    halves = tokens_part // part
    cut = values.reshape(videos, halves, size, frames, part, width)
    whole = jnp.zeros((videos, frames, size, halves, part, width), values.dtype)
    for k, block in enumerate(
        exchange_parts([cut[:, :, k] for k in range(size)], between, after)
    ):
        block = jnp.swapaxes(block, 1, 2)[:, :, None]
        whole = lax.dynamic_update_slice_in_dim(whole, block, j ^ k, axis=2)
    return whole.reshape(videos, frames, tokens, width)


def local(
    latents,
    added_noise,
    text_states,
    timesteps,
    token_counts,
    frame_counts,
    w_shared,
    w_spatial,
    w_temporal,
    shift_tables,
    m_shared,
    m_spatial,
    m_temporal,
    m_tables,
    v_shared,
    v_spatial,
    v_temporal,
    v_tables,
):
    i, j = lax.axis_index("fsdp"), lax.axis_index("frame")
    c = j % 2
    n_fsdp, n_frame = lax.axis_size("fsdp"), lax.axis_size("frame")
    rows_own = w_shared.shape[0]
    frames = latents.shape[2]
    frames_all = frames * n_frame
    videos = latents.shape[0] * latents.shape[1]
    tokens = latents.shape[3]
    texts = text_states.shape[2]

    explicit = few("fsdp")
    if explicit:
        mine = own_pieces(
            w_spatial,
            w_temporal,
            [j, jnp.where(c == 0, 4, 7), 8 + j, 12 + j],
            [j, 4 + j, 4 + (j ^ 2), 8 + j, 8 + (j ^ 2)],
        )
        first, rest = mine[:1], mine[1:]
        first_near = jnp.stack([first, swap(first, "fsdp", 2)], axis=1)

    shared_parts = split_columns(w_shared, shared_widths())
    if explicit:
        shared_parts = gate(shared_parts, [first_near])
        text_states = gate(text_states, [first_near])
    patch_own, time_one, caption_w, time_two, mod_w, final_own = shared_parts
    time_one, time_two, mod_w = [one.astype(BF16) for one in (time_one, time_two, mod_w)]
    pair_w = w_spatial[:, 5 * D : 7 * D].astype(BF16)
    steps_own = timesteps.reshape(videos)
    steps_two = jnp.concatenate([steps_own // 32, steps_own % 32]).astype(BF16)[:, None]
    small = jnp.concatenate(
        [
            patch_own.T.astype(BF16),
            final_own.T.astype(BF16),
            shift_tables.T.astype(BF16),
            jnp.broadcast_to(steps_two, (2 * videos, rows_own)),
        ]
    )
    small = jnp.pad(small, ((0, -small.shape[0] % 16), (0, 0)))
    small = collect(small, "fsdp")
    at = 2 * PCH + 14
    steps_all = small[:, at : at + 2 * videos, 0].astype(F32)
    steps_all = steps_all[:, :videos] * 32.0 + steps_all[:, videos:]
    small = jnp.swapaxes(to_relative(small, "fsdp"), 0, 1).reshape(small.shape[1], D)
    patch_w, final_w = small[:PCH], small[PCH : 2 * PCH]
    tables = small[2 * PCH : at].astype(F32)

    cond_index = jnp.where(few("fsdp"), i, 0)
    place = jnp.stack([cond_index // 2, cond_index % 2, j]).astype(jnp.int32)

    step_float = timesteps.reshape(videos).astype(F32)
    token_count = token_counts.reshape(videos)
    alpha_bar = jnp.cos((step_float / 1000.0 + 0.008) / 1.008 * (math.pi / 2)) ** 2
    snr_value = alpha_bar / (1.0 - alpha_bar)
    loss_weight = jnp.minimum(snr_value, SNR_GAMMA) / snr_value

    half_count = FREQ // 2
    frequency = jnp.exp(-math.log(10000.0) * jnp.arange(half_count, dtype=F32) / half_count)
    angles = steps_all.reshape(-1)[:, None] * frequency[None, :]
    features = jnp.concatenate([jnp.cos(angles), jnp.sin(angles)], axis=-1).astype(BF16)
    hidden_pre = dot_t(features, time_one)
    hidden_act = jax.nn.silu(hidden_pre).astype(BF16)
    embedding_all = sum_relative(dot(hidden_act, time_two).reshape(n_fsdp, videos, D), "fsdp")
    embedding = embedding_all[0]
    embedding_part = lax.dynamic_slice(
        embedding_all.reshape(-1, D), (0, i * rows_own), (n_fsdp * videos, rows_own)
    )
    embed_act = jax.nn.silu(embedding_part).astype(BF16)
    mod_half = dot(embed_act, lax.dynamic_slice(mod_w, (0, c * 3 * D), (rows_own, 3 * D)))
    mod_half = deliver(mod_half.reshape(n_fsdp, videos, 3 * D), "fsdp")
    mod_other = swap(mod_half, "frame", 1)
    modulation = jnp.concatenate(
        [jnp.where(c == 0, mod_half, mod_other), jnp.where(c == 0, mod_other, mod_half)], axis=1
    ).reshape(videos, 6, D)
    six_spatial = modulation + tables[None, 0:6]
    six_temporal = modulation + tables[None, 6:12]
    final_rows = embedding[:, None, :] + tables[None, 12:14]

    text_part = TXT_D // n_frame
    text_own = text_states.reshape(videos * texts, TXT_D)
    text_own = lax.dynamic_slice(text_own, (0, j * text_part), (videos * texts, text_part))
    text_all = collect(text_own, "fsdp").reshape(-1, text_part)
    caption_part = lax.dynamic_slice(caption_w, (0, j * text_part), (rows_own, text_part))
    caption_part = caption_part.astype(BF16)
    caption_pre = sum_over_frame_low(dot_t(text_all, caption_part))
    caption = gelu_tanh(caption_pre).astype(BF16)
    pair_part = 2 * D // n_frame
    pair_w_part = lax.dynamic_slice(pair_w, (0, j * pair_part), (rows_own, pair_part))
    pair = dot(caption, pair_w_part).astype(BF16).reshape(n_fsdp, videos * texts, pair_part)
    pair = collect(deliver(pair, "fsdp").astype(BF16), "frame")
    pair = jnp.swapaxes(to_relative(pair, "frame"), 0, 1).reshape(videos, texts, 2 * D)

    target = to_tokens(added_noise.reshape(videos, frames, tokens, PCH)).astype(F32)

    if explicit:

        def with_far(near, after):
            return jnp.concatenate([near, swap(gate(near, after), "fsdp", 4)], axis=1)

        def y(lines, after):
            return swap(gate(lines, after), "fsdp", 1)

        def x(lines, after):
            return swap(gate(lines, after), "frame", 2)

        def core(lines, after):
            return swap(gate(lines, after), "frame", 1)

        def joined(*arrays):
            return jnp.concatenate(arrays)

        done = [first_near]
        la = with_far(first_near, done)
        near_bc = jnp.stack([rest[:2], swap(gate(rest[:2], done), "fsdp", 2)], axis=1)
        done = [la, near_bc]
        lbc = with_far(near_bc, done)
        near = jnp.stack([rest[2:], swap(gate(rest[2:], done), "fsdp", 2)], axis=1)
        ya, xla = y(la, done), x(la, done)
        done = [lbc, ya, xla, near, text_all]
        lde = with_far(near[0:2], done)
        ybc, x1 = y(lbc, done), x(joined(ya, lbc[1:]), done)
        k1 = core(joined(la, xla), done)
        done = [lde, ybc, x1, k1, caption_pre, target]
        lf = with_far(near[2:4], done)
        yde, x2 = y(lde, done), x(joined(ybc[1:], lde[:1]), done)
        k2 = core(joined(ya, x1[:1], lbc, ybc), done)
        done = [lf, yde, x2, k2, pair, modulation]
        lg = with_far(near[4:6], done)
        yf, x3 = y(lf, done), x(joined(lde[1:], yde[:1]), done)
        k3 = core(joined(x1[1:], lde, x2, yde), done)
        spatial_attn = [
            ((la, 0), (ya, 0)),
            ((k1, 0), (k2, 0)),
            ((xla, 0), (x1, 0)),
            ((k1, 1), (k2, 1)),
        ]
        cross_attn = [((lbc, 0), (ybc, 0)), ((k2, 2), (k2, 4))]
    else:
        done = []
        spatial_attn = [gathered_piece(w_spatial, j ^ k) for k in range(4)]
        cross_attn = [
            gathered_piece(w_spatial, jnp.where(c == n, 4, 7)) for n in range(2)
        ]
        spatial_up, spatial_down = [
            [gathered_piece(w_spatial, base + (j ^ k)) for k in range(4)] for base in (8, 12)
        ]
        temporal_attn, temporal_up, temporal_down = [
            [gathered_piece(w_temporal, base + (j ^ k)) for k in range(4)] for base in (0, 4, 8)
        ]

    noise_own = added_noise.reshape(videos, frames * tokens, PCH)
    clean = latents.reshape(videos, frames * tokens, PCH).astype(F32)
    noisy = (
        jnp.sqrt(alpha_bar)[:, None, None] * clean
        + jnp.sqrt(1.0 - alpha_bar)[:, None, None] * noise_own.astype(F32)
    ).astype(BF16)
    start = gate(dot(noisy, patch_w), done)
    key_valid = (jnp.arange(tokens)[None, :] < token_count[:, None]).astype(F32)
    spatial_allowed = jnp.broadcast_to(key_valid[:, :, None], (videos, tokens, tokens))
    middle1, packed1, projected1, lefts1, cross_query = attention_forward(
        place, six_spatial, start, spatial_allowed, pair, spatial_attn + cross_attn
    )
    if explicit:
        done = [lg, yf, x3, k3, middle1, fence(middle1)]
        k4 = core(x3, done)
        x4 = x(yde[1:], done)
        yg = y(lg, done)
        k5 = core(joined(lf, yf), [k4])
        spatial_up = [
            ((lbc, 1), (ybc, 1)),
            ((k2, 3), (k2, 5)),
            ((x1, 1), (x2, 0)),
            ((k3, 0), (k3, 3)),
        ]
        spatial_down = [
            ((lde, 0), (yde, 0)),
            ((k3, 1), (k3, 5)),
            ((x2, 1), (x3, 1)),
            ((k3, 4), (k4, 1)),
        ]
        middle1 = gate(middle1, done)
    hidden1, normed1, ups1, active1, lowered1 = mlp_forward(
        place, six_spatial, middle1, spatial_up, spatial_down
    )

    hidden = to_tokens(
        hidden1.reshape(videos, frames, tokens, D), [x4] if explicit else []
    )
    rows = hidden.shape[1]
    part = tokens // frames_all
    clip_ends = jnp.cumsum(frame_counts.reshape(videos, -1), axis=-1)
    block_row = jnp.arange(tokens, dtype=jnp.int32)
    frame_at = ((block_row // (frames * part)) ^ j) * frames + block_row // part % frames
    segment = jnp.sum(
        (frame_at[None, :, None] >= clip_ends[:, None, :]).astype(jnp.int32), axis=-1
    )
    same_token = (block_row % part)[:, None] == (block_row % part)[None, :]
    same = same_token[None] & (segment[:, :, None] == segment[:, None, :])
    temporal_allowed = same.astype(F32)
    token_at = (
        j * (tokens // n_frame)
        + jnp.arange(rows, dtype=jnp.int32) // tokens * part
        + jnp.arange(rows, dtype=jnp.int32) % part
    )
    if explicit:
        k7 = core(x4, [])
        temporal_attn = [
            ((lde, 1), (yde, 1)),
            ((k3, 2), (k3, 6)),
            ((x3, 0), (x4, 0)),
            ((k4, 0), (k7, 0)),
        ]
        done = [k5, hidden, k7]
        k6 = core(joined(lg, yg), [hidden, yg])
        temporal_up, temporal_down = [
            [((l, 0), (b, 0)), ((k, 0), (k, 2)), ((l, 1), (b, 1)), ((k, 1), (k, 3))]
            for l, b, k in ((lf, yf, k5), (lg, yg, k6))
        ]
        hidden = gate(hidden, done)
    middle2, packed2, projected2, lefts2 = attention_forward(
        place, six_temporal, hidden, temporal_allowed, None, temporal_attn
    )
    hidden2, normed2, ups2, active2, lowered2 = mlp_forward(
        place, six_temporal, middle2, temporal_up, temporal_down
    )

    shift_final = final_rows[:, 0][:, None, :]
    scale_final = final_rows[:, 1][:, None, :]
    normed_final = modulate(hidden2, shift_final, scale_final).astype(BF16)
    predicted = dot_t(normed_final, final_w)
    pred_error = predicted - target
    keep_weight = (token_at[None, :] < token_count[:, None]).astype(F32) * loss_weight[:, None]
    keep_weight = keep_weight[:, :, None]
    loss_part = jnp.sum(keep_weight * pred_error * pred_error) / PCH
    weight_part = jnp.sum(loss_weight * token_count.astype(F32)) * frames_all

    grad_pred = (keep_weight * pred_error * (2.0 / PCH)).astype(BF16)
    grad_final_w = outer(grad_pred, normed_final)
    grad_hidden2, grad_shift_final, grad_scale_final = modulate_back(
        hidden2, shift_final, scale_final, dot(grad_pred, final_w)
    )
    slots = [(0, k) for k in range(4)]
    low2 = (grad_hidden2 * six_temporal[:, 5][:, None, :]).astype(BF16)

    def pieces_of(lefts, rights, which, after=(), added=()):
        return outer_pieces(place, gate(lefts, after), rights, which, added)

    def own_pieces_of(lefts, rights, which, after, added):
        return outer_pieces(place, gate(lefts, after), rights, which, (added,), True)

    others, mine = [slots[1], slots[3]], [slots[0], slots[2]]
    which = [((j ^ k) // 3, j ^ k) for k in range(4)]

    other1 = pieces_of(low2, active2, others)
    core1 = swap(other1, "frame", 1)
    grad_middle2, grad_ups2, six_mlp2 = mlp_backward(
        place,
        six_temporal,
        middle2,
        ups2,
        lowered2,
        gate(grad_hidden2, [other1]),
        temporal_up,
        temporal_down,
    )
    sum1 = Scatter(own_pieces_of(low2, active2, mine, [grad_middle2], core1))
    other2 = pieces_of(normed2, grad_ups2, others, [sum1.pieces])
    done = [other2]
    sum1.along_y(done)
    core2 = swap(other2, "frame", 1)
    grad_hidden, rights2, six_attn2 = attention_backward(
        place,
        six_temporal,
        hidden,
        temporal_allowed,
        packed2,
        projected2,
        gate(grad_middle2, done),
        temporal_attn,
    )
    sum2 = Scatter(own_pieces_of(normed2, grad_ups2, mine, [grad_hidden], core2))
    other3 = pieces_of(lefts2, rights2, [which[1], which[3]], [sum2.pieces])
    done = [sum1.sent, other3]
    sum2.along_y(done)
    half1 = sum1.along_z(done)
    core3 = swap(gate(other3, done), "frame", 1)
    grad_hidden1 = from_tokens(gate(grad_hidden, done), frames, [half1])
    grad_hidden1 = grad_hidden1.reshape(videos, frames * tokens, D)
    sum3 = Scatter(own_pieces_of(lefts2, rights2, [which[0], which[2]], [half1], core3))
    low1 = gate(grad_hidden1, [sum3.pieces]) * six_spatial[:, 5][:, None, :]
    low1 = low1.astype(BF16)
    other4 = pieces_of(low1, active1, others)
    done = [sum2.sent, sum1.sent, other4]
    sum3.along_y(done)
    half2, quarter1 = sum2.along_z(done), sum1.end_z(done)
    core4 = swap(gate(other4, done), "frame", 1)
    grad_middle1, grad_ups1, six_mlp1 = mlp_backward(
        place,
        six_spatial,
        middle1,
        ups1,
        lowered1,
        gate(grad_hidden1, [half2, quarter1]),
        spatial_up,
        spatial_down,
    )
    sum4 = Scatter(own_pieces_of(low1, active1, mine, [grad_middle1], core4))
    other5 = pieces_of(normed1, grad_ups1, others, [sum4.pieces])
    done = [sum3.sent, sum2.sent, sum1.sent, other5]
    sum4.along_y(done)
    half3, quarter2, rows1 = sum3.along_z(done), sum2.end_z(done), sum1.rows(done)
    core5 = swap(gate(other5, done), "frame", 1)
    grad_after1, rights7, grad_pair = cross_backward(
        place, gate(grad_middle1, [half3, quarter2]), pair, cross_query, cross_attn
    )
    sum5 = Scatter(own_pieces_of(normed1, grad_ups1, mine, [grad_after1], core5))
    other7 = pieces_of(lefts1, rights7, [(3 - c, 1 - c)], [sum5.pieces])
    done = [sum4.sent, sum3.sent, sum2.sent, other7]
    sum5.along_y(done)
    half4, quarter3, rows2 = sum4.along_z(done), sum3.end_z(done), sum2.rows(done)
    core7 = swap(gate(other7, done), "frame", 1)
    grad_start, rights1, six_attn1 = attention_backward(
        place,
        six_spatial,
        start,
        spatial_allowed,
        packed1,
        projected1,
        gate(grad_after1, [half4, quarter3]),
        spatial_attn,
    )
    other6 = pieces_of(lefts1, rights1, [which[1], which[3]], [grad_start])
    sum7 = Scatter(own_pieces_of(lefts1, rights7, [(2 + c, c)], [other6], core7))
    done = [sum5.sent, sum4.sent, sum3.sent, sum7.pieces]
    sum7.along_y(done)
    half5, quarter4, rows3 = sum5.along_z(done), sum4.end_z(done), sum3.rows(done)
    core6 = swap(gate(other6, done), "frame", 1)

    grad_pair = gate(grad_pair, [half5, quarter4]).astype(BF16)
    grad_pair = grad_pair.reshape(videos * texts, n_frame, pair_part)
    grad_pair = to_relative(jnp.swapaxes(grad_pair, 0, 1), "frame")
    six_s, six_t = [
        jnp.concatenate([attn[:, 0:3], mlp[:, 3:6]], axis=1)
        for attn, mlp in ((gate(six_attn1, [half5, quarter4]), six_mlp1), (six_attn2, six_mlp2))
    ]
    grad_final = jnp.stack([grad_shift_final, grad_scale_final], axis=1)
    grad_patch_w = outer(noisy, gate(grad_start, [half5, quarter4]).astype(BF16))
    cond = jnp.concatenate(
        [
            grad_patch_w,
            grad_final_w,
            jnp.sum(jnp.concatenate([six_s, six_t, grad_final], axis=1), axis=0),
            jnp.concatenate([six_s + six_t, grad_final], axis=1).reshape(-1, D),
        ]
    )
    pair_core = swap(jnp.stack([grad_pair[1], grad_pair[3]]), "frame", 1)
    cond_core = swap(cond, "frame", 1)
    sum6 = Scatter(
        own_pieces_of(lefts1, rights1, [which[0], which[2]], [half5, quarter4], core6)
    )
    done = [sum6.pieces, sum7.sent, sum4.sent, pair_core, cond_core]
    sum6.along_y(done)
    half7, rows4 = sum7.along_z(done), sum4.rows(done)
    pair_core, cond_core = gate((pair_core, cond_core), done)
    pair_x = swap(plus(grad_pair[2], pair_core[1]), "frame", 2)
    cond = cond + cond_core
    cond_x = swap(cond, "frame", 2)
    done = [pair_x, cond_x, half7]
    pair_x, cond_x = gate((pair_x, cond_x), done)
    grad_pair = plus(plus(grad_pair[0], pair_core[0]), pair_x)
    cond = cond + cond_x
    small_grad = jnp.swapaxes(cond[: 2 * PCH + 14].reshape(-1, n_fsdp, rows_own), 0, 1)
    small_grad = Deliver(to_relative(small_grad, "fsdp"))
    cond_rows = 8 * videos
    sent = Collect(
        jnp.concatenate([cond[2 * PCH + 14 :].astype(BF16), grad_pair.reshape(-1, D)])
    )
    early = jnp.concatenate([rows1, rows2, rows3])
    crossed = swap(
        gate(jnp.concatenate([rows1[::-1], rows2[::-1], rows3[::-1]]), [cond]), "frame", 2
    )
    small_sent = sent.sent + small_grad.sent if explicit else [cond]
    done = small_sent + [sum6.sent, sum5.sent, crossed]
    half6 = sum6.along_z(done)
    sent.beside([half6])
    small_grad.beside([half6])
    quarter5 = sum5.end_z([half6])
    early = plus(early, gate(crossed, [half6]))
    early_other = swap(early, "frame", 1)
    received = sent.all([quarter5, early])
    small_grad = small_grad.total([quarter5, early]).T
    quarter7, rows5 = sum7.end_z([received]), sum5.rows([received])
    late = jnp.concatenate([rows4, rows5])
    grad_pair = received[:, cond_rows:].reshape(-1, pair_part)
    pair_w_grad = outer(caption, grad_pair)
    grad_caption = sum_over_frame_low(dot_t(grad_pair, pair_w_part))
    cond = received[:, :cond_rows].reshape(n_fsdp * videos, 8, D)
    grad_mod = cond[:, :6].reshape(-1, 6 * D)
    mod_grad = outer(embed_act, grad_mod)
    final_part = lax.dynamic_slice(
        cond[:, 6].astype(F32) + cond[:, 7].astype(F32), (0, i * rows_own), embedding_part.shape
    )
    grad_embed = (
        jax.vjp(jax.nn.silu, embedding_part)[1](dot_t(grad_mod, mod_w))[0] + final_part
    ).astype(BF16)
    grad_embed = Collect(grad_embed.reshape(n_fsdp, videos, rows_own))
    late_x = swap(
        gate(jnp.concatenate([rows4[::-1], rows5[::-1]]), [grad_caption]), "frame", 2
    )
    quarter6 = sum6.end_z([grad_caption, quarter7])
    grad_caption = gate(grad_caption, [quarter6])
    grad_caption = jax.vjp(gelu_tanh, caption_pre)[1](grad_caption)[0].astype(BF16)
    both = jnp.concatenate([outer(grad_caption, text_all), pair_w_grad], axis=1).astype(BF16)
    late = plus(late, gate(late_x, [both]))
    late_other = swap(late, "frame", 1)
    both = jnp.stack([both, swap(both, "frame", 1)])
    rows7 = sum7.rows([quarter6])
    rows6 = sum6.rows([both])
    last = plus(
        jnp.concatenate([rows6, rows7]),
        swap(jnp.concatenate([rows6[::-1], rows7]), "frame", 2),
    )
    both = jnp.concatenate([both, swap(gate(both, [rows6]), "frame", 2)])
    grad_embed.beside([quarter6])
    received = grad_embed.all([rows6])
    last_other = swap(last, "frame", 1)
    both = to_relative(both, "frame")
    caption_grad, pair_w_grad = [
        jnp.swapaxes(one, 0, 1).reshape(rows_own, -1)
        for one in (both[:, :, :text_part], both[:, :, text_part:])
    ]
    step = np.arange(n_fsdp)
    grad_embed = received[step[:, None], step[:, None] ^ step[None, :]]
    grad_embed = jnp.transpose(to_relative(grad_embed, "fsdp"), (1, 2, 0, 3)).reshape(-1, D)
    time_two_grad = outer(hidden_act, grad_embed)
    grad_hidden = dot_t(grad_embed, time_two)
    grad_hidden = jax.vjp(jax.nn.silu, hidden_pre)[1](grad_hidden)[0].astype(BF16)
    time_one_grad = outer(grad_hidden, features)
    shared_grads = jnp.concatenate(
        [
            small_grad[:, :PCH].astype(BF16),
            time_one_grad.astype(BF16),
            caption_grad,
            time_two_grad.astype(BF16),
            mod_grad.astype(BF16),
            small_grad[:, PCH : 2 * PCH].astype(BF16),
        ],
        axis=1,
    )

    pair_pieces = jnp.stack([pair_w_grad[:, :D], pair_w_grad[:, D:]])
    tables_grad = small_grad[:, 2 * PCH :]
    relative = np.arange(4) ^ j
    odd, half = relative % 2, relative // 2
    core_first = jnp.stack([c, 1 - c])
    temporal_arrays = [early, early_other]
    temporal_source = jnp.concatenate([odd, odd, odd]).astype(jnp.int32)
    temporal_entry = jnp.concatenate([4 + half, 2 + half, half]).astype(jnp.int32)
    spatial_arrays = [last, last_other, late, late_other, pair_pieces]
    fours = jnp.array([4, 4], jnp.int32)
    spatial_source = jnp.concatenate(
        [odd, core_first[:1], fours, core_first[1:], 2 + odd, 2 + odd]
    ).astype(jnp.int32)
    spatial_entry = jnp.concatenate(
        [half, fours[:1] // 2, fours // 4 - np.array([1, 0]), fours[:1] // 2, 2 + half, half]
    ).astype(jnp.int32)

    def squares(values, axes=None):
        values = values.astype(F32)
        return jnp.sum(values * values, axis=axes)

    def piece_squares(arrays, source, entry):
        most = max(one.shape[0] for one in arrays)
        table = jnp.concatenate(
            [jnp.pad(squares(one, (1, 2)), (0, most - one.shape[0])) for one in arrays]
        )
        return table[source * most + entry]

    def rows_of(widths, first):
        which = np.repeat(np.arange(len(widths)) + first, widths)
        return jnp.asarray(which)[None, :] == jnp.arange(18)[:, None]

    shared_rows = rows_of(shared_widths(), 0)
    spatial_rows = rows_of([width // D for width in spatial_widths()], 6)
    temporal_rows = rows_of([width // D for width in temporal_widths()], 13)

    def matrix_sums(shared, spatial, temporal, table):
        totals = jnp.where(jnp.arange(18) == 17, table, 0.0)
        for marks, values in (
            (shared_rows, shared),
            (spatial_rows, spatial),
            (temporal_rows, temporal),
        ):
            totals = totals + jnp.sum(jnp.where(marks, values[None, :], 0.0), axis=1)
        return totals

    def spread(marks, values):
        return jnp.sum(jnp.where(marks, values[:, None], 0.0), axis=0)

    grad_part_sq = matrix_sums(
        squares(shared_grads, 0),
        piece_squares(spatial_arrays, spatial_source, spatial_entry),
        piece_squares(temporal_arrays, temporal_source, temporal_entry),
        squares(tables_grad),
    )
    loss_all = sum_over(loss_part[None], "frame")
    numbers = sum_over(jnp.concatenate([grad_part_sq, loss_all, weight_part[None]]), "fsdp")
    grad_sq, loss_sum, weight_total = numbers[:18], numbers[18], numbers[19]
    grad_norm = jnp.sqrt(jnp.sum(grad_sq)) / weight_total
    factor = CLIP_NORM / jnp.maximum(grad_norm, CLIP_NORM)
    grad_scale = factor / weight_total
    scale = grad_scale[None]
    shared_new = row_moments(scale, shared_grads, m_shared, v_shared, w_shared)
    spatial_new = moments(
        spatial_arrays, spatial_source, spatial_entry, scale, m_spatial, v_spatial, w_spatial
    )
    temporal_new = moments(
        temporal_arrays, temporal_source, temporal_entry, scale, m_temporal, v_temporal, w_temporal
    )
    tables_new = optimizer_step(tables_grad * grad_scale, m_tables, v_tables, shift_tables)
    spatial_sq = jnp.sum(spatial_new[3], axis=2)
    temporal_sq = jnp.sum(temporal_new[3], axis=2)
    numbers = [
        matrix_sums(shared_new[3][n], spatial_sq[:, n], temporal_sq[:, n], squares(table))
        for n, table in enumerate((tables_new[2], shift_tables))
    ]
    numbers = sum_over(jnp.concatenate(numbers), "fsdp")
    update_sq, weight_sq = numbers[:18], numbers[18:]
    trust = LEARN_RATE * jnp.sqrt(weight_sq) / jnp.sqrt(update_sq)
    new_shared, copy_shared = apply_update(
        spread(shared_rows, trust)[None], w_shared, shared_new[2]
    )
    new_spatial, copy_spatial = apply_update(
        spread(spatial_rows, trust), w_spatial, spatial_new[2]
    )
    new_temporal, copy_temporal = apply_update(
        spread(temporal_rows, trust), w_temporal, temporal_new[2]
    )
    new_tables = shift_tables - trust[17] * tables_new[2]
    return (
        loss_sum,
        weight_total,
        grad_norm,
        jnp.stack([jnp.sqrt(weight_sq), jnp.sqrt(update_sq)]),
        jnp.sqrt(grad_sq) * grad_scale,
        new_shared,
        new_spatial,
        new_temporal,
        new_tables,
        shared_new[0],
        spatial_new[0],
        temporal_new[0],
        tables_new[0],
        shared_new[1],
        spatial_new[1],
        temporal_new[1],
        tables_new[1],
        copy_shared,
        copy_spatial,
        copy_temporal,
        new_tables.astype(BF16),
    )


def solution(mesh):
    rows = P("fsdp", None)
    return jax.shard_map(
        local,
        mesh=mesh,
        in_specs=(
            P(None, "fsdp", "frame", None, None),
            P(None, "fsdp", "frame", None, None),
            P(None, "fsdp", None, None),
            P(None, "fsdp"),
            P(None, "fsdp"),
            P(None, "fsdp", None),
        )
        + (rows,) * 12,
        out_specs=(P(),) * 5 + (rows,) * 16,
        check_vma=False,
    )
```
